32 devices in a mesh: region: 4 (over x, core), dev: 8 (over z, y).
Axes of the slice: x: 2, y: 2, z: 4, core: 2. Of those that a mesh axis runs over, the one named last changes fastest.
Arguments:
- tile_values: bfloat16 [2048, 3, 128, 128], P(('region', 'dev')), as said below
- basis_tiles: bfloat16 [2048, 128, 128], P(('region', 'dev')), may hold values from -0.09375 to 0.09375
- tile_offsets: int32 [2048, 2], replicated, may hold values from -2 to 2, as said below
- aggregate_ids: int32 [2048], replicated, may hold values from 0 to 95, as said below
Outputs:
- prolongator: bfloat16 [2048, 3, 128, 128], P(('region', 'dev'))
- coarse_tiles: bfloat16 [128, 3, 128, 128], P('dev')
The draws below stay inside these ranges and needn't reach their ends.
Inputs may be any that keep to these rules, and one draw needn't show every extreme that they name: `tile_offsets`: each block's two offsets are distinct and point to a block inside the 2048 blocks. `aggregate_ids`: aggregates are runs of whole units of 8 consecutive blocks inside one device's 64 blocks; ids count up from 0 along the blocks without gaps; each device holds 2 to 4 aggregates, some device exactly 4; the devices of block ranges 2i and 2i + 1 together hold 6 aggregates. `tile_values`: the diagonal entries of tile 0 of every block lie between 1.5 and 4.5.
All inputs are finite; a program needn't handle non-finite values.
Results may differ from the reference program's by a relative error of at most 0.0031.
Values may be sent and summed in bfloat16 or wider, within the bound.
No kernel may reach another device: no remote copies, remote signals or barrier semaphores. Data moves between devices by JAX's collectives and lax.ppermute only.
A program may use at most 192 MiB of HBM per device.

```python
import math
import jax
import jax.numpy as jnp
from jax import lax

B = 128
CW = 128
R = 64
GRP = 8
MOSTA = 4
NB = 2048
N_REGION = 4
N_DEV = 8


def draw_tile_values(key, part):
    key_noise, key_diag = jax.random.split(key)
    tile_shape = (NB, 3, B, B)
    noise_part = jax.random.normal(key_noise, tile_shape, jnp.float32) / math.sqrt(B)
    diagonal = jax.random.uniform(key_diag, (NB, B), jnp.float32, 2.0, 4.0)
    identity = jnp.eye(B, dtype=jnp.float32)
    leading = noise_part[:, 0] * (1.0 - identity) + diagonal[:, :, None] * identity
    return noise_part.at[:, 0].set(leading).astype(jnp.bfloat16)


def draw_tile_offsets(key, part):
    candidates = jnp.array([-2, -1, 1, 2], jnp.int32)
    scores = jax.random.randint(key, (NB, 4), 0, 4096) * 4 + jnp.arange(4, dtype=jnp.int32)
    targets = jnp.arange(NB, dtype=jnp.int32)[:, None] + candidates
    allowed = (targets >= 0) & (targets < NB)
    scores = jnp.where(allowed, scores, -1)
    ignored, picked = lax.top_k(scores, 2)
    return candidates[picked].astype(jnp.int32)


def draw_aggregate_ids(key, part):
    unit_total = R // GRP
    devices_total = NB // R
    pair_total = devices_total // 2
    lowest = unit_total // 4
    highest = unit_total // 2
    key_count, key_pick, key_cut = jax.random.split(key, 3)
    first_counts = jax.random.randint(key_count, (pair_total,), lowest, highest + 1)
    chosen = jax.random.randint(key_pick, (), 0, pair_total)
    first_counts = jnp.where(jnp.arange(pair_total, dtype=jnp.int32) == chosen, highest, first_counts)
    second_counts = lowest + highest - first_counts
    counts = jnp.stack([first_counts, second_counts], axis=1).reshape(-1).astype(jnp.int32)
    scores = jax.random.randint(key_cut, (devices_total, unit_total - 1), 0, 4096) * unit_total + jnp.arange(unit_total - 1, dtype=jnp.int32)
    sort_order = jnp.argsort(-scores, axis=1)
    rank_values = jnp.argsort(sort_order, axis=1)
    cut_flags = (rank_values < counts[:, None] - 1).astype(jnp.int32)
    within = jnp.concatenate([jnp.zeros((devices_total, 1), jnp.int32), jnp.cumsum(cut_flags, axis=1)], axis=1)
    starts = jnp.cumsum(counts) - counts
    unit_ids = starts[:, None] + within
    return jnp.repeat(unit_ids.reshape(-1), GRP).astype(jnp.int32)


def steps_of(stream_key, shape, cuts, smallest, high):
    factor_of, own = 1.0, jax.random.fold_in(stream_key, 6)
    for position, parts in cuts:
        draws = jnp.exp(jax.random.uniform(jax.random.fold_in(own, position), (parts,), jnp.float32, smallest / len(cuts), high / len(cuts)))
        factor_of = factor_of * jnp.repeat(draws, shape[position] // parts).reshape([-1 if axis == position else 1 for axis in range(len(shape))])
    return factor_of


def normal_values(stream_key, shape, scale, bound, cuts=(), kind=jnp.bfloat16):
    loudness = steps_of(stream_key, shape, cuts, -0.22, 0.18) if cuts else 1.0
    values = jax.random.normal(stream_key, shape, jnp.float32) * scale * loudness
    return jnp.minimum(jnp.maximum(values, -bound), bound).astype(kind)


def setup_inputs(seed: int = 0) -> dict:
    seeds = jax.random.split(jax.random.key(seed), 5)
    return {
        "tile_values": draw_tile_values(jax.random.fold_in(seeds[4], 71), 0),
        "basis_tiles": normal_values(seeds[1], (NB, B, CW), (4 * B * GRP) ** -0.5, 0.09375, ((0, 32),)),
        "tile_offsets": draw_tile_offsets(jax.random.fold_in(seeds[4], 71), 0),
        "aggregate_ids": draw_aggregate_ids(jax.random.fold_in(seeds[4], 71), 0),
    }


damping = 0.6


def place_terms(tile_block, offset_block, neighbour_prol, neighbour_offsets, own_prol):
    slot_index = offset_block[:, :, None] + neighbour_offsets + 4
    one_hot = (slot_index[..., None] == jnp.arange(9, dtype=jnp.int32)).astype(jnp.float32)
    products = jnp.einsum('pkij,pkqjc->pkqic', tile_block.astype(jnp.float32), neighbour_prol.astype(jnp.float32))
    band_rows = jnp.einsum('pkqs,pkqic->psic', one_hot, products, precision=lax.Precision.HIGHEST).astype(jnp.bfloat16)
    return jnp.einsum('pkic,psid->pkscd', own_prol.astype(jnp.float32), band_rows.astype(jnp.float32))


def reference(tile_values, basis_tiles, tile_offsets, aggregate_ids):
    block_count = tile_values.shape[0]
    steps_count = block_count // R
    leading = jnp.zeros((block_count, 1), jnp.int32)
    full_offsets = jnp.concatenate([leading, tile_offsets], axis=1)
    padded_offsets = jnp.pad(full_offsets, ((8, 8), (0, 0)))
    padded_basis = jnp.pad(basis_tiles, ((2, 2), (0, 0), (0, 0)))
    row_span = jnp.arange(R, dtype=jnp.int32)

    def prol_block(block_id):
        begin_row = (block_id * R).astype(jnp.int32)
        tile_block = lax.dynamic_slice_in_dim(tile_values, begin_row, R, 0).astype(jnp.float32)
        offset_block = lax.dynamic_slice_in_dim(full_offsets, begin_row, R, 0)
        near_index = (begin_row + row_span[:, None] + 2 + offset_block).astype(jnp.int32)
        neighbour_basis = padded_basis[near_index].astype(jnp.float32)
        product = jnp.einsum('pkij,pkjc->pkic', tile_block, neighbour_basis)
        inverse_diag = 1.0 / jnp.diagonal(tile_block[:, 0], axis1=1, axis2=2)
        own_basis = lax.dynamic_slice_in_dim(basis_tiles, begin_row, R, 0).astype(jnp.float32)
        identity_part = jnp.zeros_like(product).at[:, 0].set(own_basis)
        return (identity_part - damping * inverse_diag[:, None, :, None] * product).astype(jnp.bfloat16)

    prolongator = lax.map(prol_block, jnp.arange(steps_count, dtype=jnp.int32)).reshape(block_count, 3, B, CW)
    padded_prol = jnp.pad(prolongator, ((2, 2), (0, 0), (0, 0), (0, 0)))
    slot_count = steps_count * MOSTA
    band_span = jnp.arange(9, dtype=jnp.int32) - 4

    def coarse_block(coarse, block_id):
        begin_row = (block_id * R).astype(jnp.int32)
        tile_block = lax.dynamic_slice_in_dim(tile_values, begin_row, R, 0)
        offset_block = lax.dynamic_slice_in_dim(full_offsets, begin_row, R, 0)
        near_index = (begin_row + row_span[:, None] + 2 + offset_block).astype(jnp.int32)
        neighbour_prol = padded_prol[near_index]
        neighbour_offsets = padded_offsets[near_index + 6]
        own_prol = lax.dynamic_slice_in_dim(prolongator, begin_row, R, 0)
        terms = place_terms(tile_block, offset_block, neighbour_prol, neighbour_offsets, own_prol)
        global_rows = begin_row + row_span
        fine_rows = (global_rows[:, None] + offset_block).astype(jnp.int32)
        fine_cols = jnp.clip(global_rows[:, None] + band_span, 0, block_count - 1).astype(jnp.int32)
        row_aggs = aggregate_ids[fine_rows]
        col_aggs = aggregate_ids[fine_cols]
        owners = (fine_rows // R).astype(jnp.int32)
        positions = owners * MOSTA + row_aggs - aggregate_ids[owners * R]
        bands = col_aggs[:, None, :] - row_aggs[:, :, None] + 1
        positions = jnp.broadcast_to(positions[:, :, None], bands.shape)
        coarse = coarse.at[positions.reshape(-1), bands.reshape(-1)].add(terms.reshape(-1, CW, CW))
        return coarse, None

    coarse_sum, ignored = lax.scan(coarse_block, jnp.zeros((slot_count, 3, CW, CW), jnp.float32), jnp.arange(steps_count, dtype=jnp.int32))
    coarse_sum = coarse_sum.reshape(N_REGION, N_DEV, MOSTA, 3, CW, CW).transpose(1, 0, 2, 3, 4, 5)
    coarse_tiles = coarse_sum.reshape(N_DEV * N_REGION * MOSTA, 3, CW, CW).astype(jnp.bfloat16)
    return prolongator, coarse_tiles
```

```python
import functools

import jax
import jax.numpy as jnp
from jax import lax
from jax.experimental import pallas as pl
from jax.experimental.pallas import tpu as pltpu
from jax.sharding import PartitionSpec as P

MOSTA = 4
GRP = 8
HALF = 4
damping = 0.6
f32, bf16 = jnp.float32, jnp.bfloat16
AXES = ("region", "dev")


def row_scale(diagonal_tile):
    size = diagonal_tile.shape[0]
    on = lax.broadcasted_iota(jnp.int32, (size, size), 0) == lax.broadcasted_iota(
        jnp.int32, (size, size), 1
    )
    diag = jnp.sum(jnp.where(on, diagonal_tile.astype(f32), 0.0), axis=1, keepdims=True)
    return damping * (1.0 / jnp.where(diag == 0.0, 1.0, diag))


def dot(a, b):
    return jnp.dot(a, b, preferred_element_type=f32)


def dot_t(a, b):
    return lax.dot_general(a, b, (((0,), (0,)), ((), ())), preferred_element_type=f32)


def tall(blocks):
    return jnp.concatenate(blocks, axis=0)


def wide(blocks):
    return jnp.concatenate(blocks, axis=1)


def smooth_row(tiles, near):
    scale = row_scale(tiles[0])
    head = near[0].astype(f32) - scale * dot(tiles[0], near[0])
    rest = [-(scale * dot(tiles[k], near[k])) for k in (1, 2)]
    return [x.astype(bf16) for x in (head, *rest)]


def edges_kernel(rows, offs, tiles_hbm, basis_hbm, low_ref, high_ref, tiles, basis, sems):
    own = (lax.axis_index("region") * lax.axis_size("dev") + lax.axis_index("dev")) * rows
    copies = [
        pltpu.make_async_copy(tiles_hbm.at[pl.ds(0, 4)], tiles.at[pl.ds(0, 4)], sems.at[0]),
        pltpu.make_async_copy(basis_hbm.at[pl.ds(0, 6)], basis.at[pl.ds(0, 6)], sems.at[1]),
        pltpu.make_async_copy(tiles_hbm.at[pl.ds(rows - 4, 4)], tiles.at[pl.ds(4, 4)], sems.at[2]),
        pltpu.make_async_copy(basis_hbm.at[pl.ds(rows - 6, 6)], basis.at[pl.ds(6, 6)], sems.at[3]),
    ]
    for c in copies:
        c.start()
    for side, out in enumerate((low_ref, high_ref)):
        copies[2 * side].wait()
        copies[2 * side + 1].wait()
        for i in range(4):
            m = i if side == 0 else rows - 4 + i
            at = i if side == 0 else i + 2
            near, weights = [basis[6 * side + at]], []
            for k in range(2):
                n = at + offs[k, own + m]
                weights.append(jnp.where((n >= 0) & (n <= 5), 1.0, 0.0).astype(f32))
                near.append(basis[6 * side + jnp.clip(n, 0, 5)])
            p0, p1, p2 = smooth_row([tiles[4 * side + i, k] for k in range(3)], near)
            total = p0.astype(f32) + weights[0] * p1.astype(f32) + weights[1] * p2.astype(f32)
            out[6 + i] = total.astype(bf16)
        for i in range(2):
            e = i if side == 0 else i + 2
            for k in range(3):
                out[3 * i + k] = tiles[4 * side + e, k]
            out[10 + i] = basis[i if side == 0 else 10 + i]


def interior_kernel(
    rows, offs, aggs, tiles_hbm, basis_hbm, prol_hbm, early_ref, mid_ref, pc_ref,
    tiles, basis, prol, cols, acc, tile_sems, basis_sem, out_sems,
):
    own = (lax.axis_index("region") * lax.axis_size("dev") + lax.axis_index("dev")) * rows
    units = rows // GRP
    base = aggs[own]
    count = aggs[own + rows - 1] - base + 1

    def tile_copy(u):
        part = pl.ds(u * GRP, GRP)
        return pltpu.make_async_copy(tiles_hbm.at[part], tiles.at[part], tile_sems.at[u])

    def out_copy(u):
        part = pl.ds(u * GRP, GRP)
        return pltpu.make_async_copy(prol.at[part], prol_hbm.at[part], out_sems.at[u])

    basis_copy = pltpu.make_async_copy(basis_hbm, basis, basis_sem)
    basis_copy.start()
    for u in range(units):
        tile_copy(u).start()
    acc[...] = jnp.zeros_like(acc)
    basis_copy.wait()

    def agg_of(m):
        return aggs[own + m]

    def near_of(m):
        return [m] + [jnp.clip(m + offs[k, own + m], 0, rows - 1) for k in range(2)]

    def smooth(u):
        mine = agg_of(u * GRP)
        slot = lax.rem(mine, 2)
        for i in range(GRP):
            m = u * GRP + i
            n = near_of(m)
            row = smooth_row([tiles[m, k] for k in range(3)], [basis[x] for x in n])
            for k in range(3):
                prol[m, k] = row[k]
            p0, p1, p2 = [x.astype(f32) for x in row]
            if 2 <= i < GRP - 2:
                cols[m, slot] = (p0 + p1 + p2).astype(bf16)
                cols[m, 1 - slot] = jnp.zeros_like(row[0])
            else:
                w1, w2 = [jnp.where(agg_of(x) == mine, 1.0, 0.0).astype(f32) for x in n[1:]]
                cols[m, slot] = (p0 + w1 * p1 + w2 * p2).astype(bf16)
                cols[m, 1 - slot] = ((1.0 - w1) * p1 + (1.0 - w2) * p2).astype(bf16)

    def gather_half(h, columns_of):
        left, right = [], []
        for i in range(HALF):
            m = h * HALF + i
            n = near_of(m)
            lhs = wide([tiles[m, k] for k in range(3)])
            right.append(dot(lhs, tall([columns_of(x) for x in n])).astype(bf16))
            left.append(columns_of(m))
        return dot_t(tall(left), tall(right))

    def half(h):
        low = agg_of(h * HALF - jnp.where(lax.rem(h, 2) == 0, 1, 0))
        high = agg_of(h * HALF + jnp.where(lax.rem(h, 2) == 0, 0, HALF))

        @pl.when(low == high)
        def _():
            slot = lax.rem(low, 2)
            acc[low - base, 1] += gather_half(h, lambda x: cols[x, slot])

        @pl.when(low != high)
        def _():
            size = tiles.shape[-1]
            added = gather_half(h, lambda x: wide([cols[x, 0], cols[x, 1]]))
            at = [jnp.where(lax.rem(low, 2) == s, low, high) for s in range(2)]
            for r in range(2):
                for s in range(2):
                    acc[at[r] - base, at[s] - at[r] + 1] += added[
                        r * size : (r + 1) * size, s * size : (s + 1) * size
                    ]

    def unit(u, carry):
        tile_copy(u).wait()
        smooth(u)
        out_copy(u).start()

        @pl.when(u > 0)
        def _():
            half(2 * u - 1)
            half(2 * u)

        return carry

    lax.fori_loop(0, units, unit, 0)
    first_slot, last_slot = lax.rem(base, 2), lax.rem(agg_of(rows - 1), 2)
    for i in range(4):
        pc_ref[i] = cols[2 + i, first_slot]
        pc_ref[4 + i] = cols[rows - 6 + i, last_slot]
    early_ref[0] = acc[0, 2].astype(bf16)
    early_ref[7] = acc[count - 1, 0].astype(bf16)
    for j in (1, 2):
        kept = jnp.where(j < count - 1, 1.0, 0.0).astype(f32)
        for b in range(3):
            early_ref[3 * j - 2 + b] = (kept * acc[j, b]).astype(bf16)
    mid_ref[0] = acc[0, 1]
    mid_ref[1] = acc[count - 1, 1]
    for u in range(units):
        out_copy(u).wait()


def rim_kernel(
    rows, total, offs, low_ref, high_ref, tiles_hbm, basis_hbm, pc_ref, mid_ref, prol_in,
    prol_hbm, late_ref, tiles, basis, prol, cols, sems,
):
    own = (lax.axis_index("region") * lax.axis_size("dev") + lax.axis_index("dev")) * rows
    size = tiles.shape[-1]
    copies = [
        pltpu.make_async_copy(tiles_hbm.at[pl.ds(0, 4)], tiles.at[0, pl.ds(2, 4)], sems.at[0]),
        pltpu.make_async_copy(basis_hbm.at[pl.ds(0, 4)], basis.at[0, pl.ds(2, 4)], sems.at[1]),
        pltpu.make_async_copy(tiles_hbm.at[pl.ds(rows - 4, 4)], tiles.at[1, pl.ds(0, 4)], sems.at[2]),
        pltpu.make_async_copy(basis_hbm.at[pl.ds(rows - 4, 4)], basis.at[1, pl.ds(0, 4)], sems.at[3]),
    ]
    for c in copies:
        c.start()
    outs = []
    for side, got in enumerate((low_ref, high_ref)):
        start = -2 if side == 0 else rows - 4
        theirs = (0, 1) if side == 0 else (4, 5)
        mine = (2, 3) if side == 0 else (2, 3)
        plain = (4, 5) if side == 0 else (0, 1)
        for i, e in enumerate(theirs):
            for k in range(3):
                tiles[side, e, k] = got[3 * i + k]
            basis[side, e] = got[10 + i]
        copies[2 * side].wait()
        copies[2 * side + 1].wait()
        nb, me = (0, 1) if side == 0 else (1, 0)
        zero = jnp.zeros((size, size), bf16)

        def near_of(e):
            m = own + start + e
            inside = (m >= 0) & (m < total)
            at = jnp.clip(m, 0, total - 1)
            return [e] + [e + jnp.where(inside, offs[k, at], 0) for k in range(2)]

        def is_mine(e):
            return (e >= 2) if side == 0 else (e <= 3)

        for i in range(4):
            e = i - 2 if side == 0 else i + 4
            cols[side, 2 + e, :, nb * size : (nb + 1) * size] = got[6 + i]
            if not 0 <= e <= 5 or e not in theirs:
                cols[side, 2 + e, :, me * size : (me + 1) * size] = zero
            e = i + 4 if side == 0 else i - 2
            cols[side, 2 + e, :, me * size : (me + 1) * size] = pc_ref[4 * side + i]
            cols[side, 2 + e, :, nb * size : (nb + 1) * size] = zero
        for e in mine:
            n = near_of(e)
            row = smooth_row([tiles[side, e, k] for k in range(3)], [basis[side, jnp.clip(x, 0, 5)] for x in n])
            for k in range(3):
                prol[side, e - 2, k] = row[k]
            p0, p1, p2 = [x.astype(f32) for x in row]
            w1, w2 = [jnp.where(is_mine(x), 1.0, 0.0).astype(f32) for x in n[1:]]
            cols[side, 2 + e, :, me * size : (me + 1) * size] = (p0 + w1 * p1 + w2 * p2).astype(bf16)
            cols[side, 2 + e, :, nb * size : (nb + 1) * size] = ((1.0 - w1) * p1 + (1.0 - w2) * p2).astype(bf16)
        out = pltpu.make_async_copy(
            prol.at[side], prol_hbm.at[pl.ds(0 if side == 0 else rows - 2, 2)], sems.at[4 + side]
        )
        out.start()
        outs.append(out)
        for e in theirs:
            n = near_of(e)
            row = smooth_row([tiles[side, e, k] for k in range(3)], [basis[side, jnp.clip(x, 0, 5)] for x in n])
            p0, p1, p2 = [x.astype(f32) for x in row]
            w1, w2 = [jnp.where(is_mine(x), 1.0, 0.0).astype(f32) for x in n[1:]]
            cols[side, 2 + e, :, me * size : (me + 1) * size] = (w1 * p1 + w2 * p2).astype(bf16)
        left, right = [], []
        for e in range(6):
            n = near_of(e)
            lhs = wide([tiles[side, e, k] for k in range(3)])
            right.append(dot(lhs, tall([cols[side, 2 + x] for x in n])).astype(bf16))
            left.append(cols[side, 2 + e, :, me * size : (me + 1) * size])
        added = dot_t(tall(left), tall(right))
        if side == 0:
            late_ref[0] = added[:, :size].astype(bf16)
            late_ref[1] = (added[:, size:] + mid_ref[0]).astype(bf16)
        else:
            late_ref[2] = (added[:, :size] + mid_ref[1]).astype(bf16)
            late_ref[3] = added[:, size:].astype(bf16)
    for out in outs:
        out.wait()


def place_kernel(rows, aggs, *refs):
    out = refs[-1]
    region, dev = lax.axis_index("region"), lax.axis_index("dev")
    for j in range(4):
        late, early = refs[2 * j], refs[2 * j + 1]
        source = lax.bitwise_xor(region, j)
        own = (source * lax.axis_size("dev") + dev) * rows
        count = aggs[own + rows - 1] - aggs[own] + 1
        at = source * MOSTA
        out[at, 0] = late[0]
        out[at, 1] = late[1]
        out[at, 2] = early[0]
        for b in range(3):
            out[at + 1, b] = early[1 + b]
            out[at + 2, b] = early[4 + b]
            out[at + 3, b] = jnp.zeros_like(early[0])
        out[at + count - 1, 0] = early[7]
        out[at + count - 1, 1] = late[2]
        out[at + count - 1, 2] = late[3]


VM = pl.BlockSpec(memory_space=pltpu.VMEM)
SM = pl.BlockSpec(memory_space=pltpu.SMEM)
ANY = pl.BlockSpec(memory_space=pl.ANY)
DMA = pltpu.SemaphoreType.DMA


def cost(products, bytes_accessed):
    return pl.CostEstimate(flops=2 * 128**3 * products, bytes_accessed=bytes_accessed, transcendentals=0)


def exchange(block):
    count = lax.axis_size("region")
    across = lax.ppermute(block, "region", [(i, i ^ 2) for i in range(count)])
    beside = lax.ppermute(block, "region", [(i, i ^ 1) for i in range(count)])
    both = lax.ppermute(across, "region", [(i, i ^ 1) for i in range(count)])
    return block, beside, across, both


def local(tile_values, basis_tiles, tile_offsets, aggregate_ids):
    rows, _, size, width = tile_values.shape
    total = tile_offsets.shape[0]
    offs = tile_offsets.T
    params = pltpu.CompilerParams(vmem_limit_bytes=56 * 2**20)
    block = (size, width)
    sds = jax.ShapeDtypeStruct
    low, high = pl.pallas_call(
        functools.partial(edges_kernel, rows),
        out_shape=[sds((12, *block), bf16)] * 2,
        in_specs=[SM, ANY, ANY],
        out_specs=[VM, VM],
        scratch_shapes=[pltpu.VMEM((8, 3, *block), bf16), pltpu.VMEM((12, *block), bf16), DMA((4,))],
        compiler_params=pltpu.CompilerParams(vmem_limit_bytes=16 * 2**20),
        cost_estimate=cost(24, 2 * 10**6),
        name="edges",
    )(offs, tile_values, basis_tiles)
    devices = lax.axis_size(AXES)
    from_low = lax.ppermute(high, AXES, [(i, i + 1) for i in range(devices - 1)])
    from_high = lax.ppermute(low, AXES, [(i + 1, i) for i in range(devices - 1)])
    prol, early, mid, pc = pl.pallas_call(
        functools.partial(interior_kernel, rows),
        out_shape=[sds((rows, 3, *block), bf16), sds((8, *block), bf16), sds((2, *block), f32), sds((8, *block), bf16)],
        in_specs=[SM, SM, ANY, ANY],
        out_specs=[ANY, VM, VM, VM],
        scratch_shapes=[
            pltpu.VMEM((rows, 3, *block), bf16),
            pltpu.VMEM((rows, *block), bf16),
            pltpu.VMEM((rows, 3, *block), bf16),
            pltpu.VMEM((rows, 2, *block), bf16),
            pltpu.VMEM((MOSTA, 3, *block), f32),
            DMA((rows // GRP,)),
            DMA,
            DMA((rows // GRP,)),
        ],
        compiler_params=params,
        cost_estimate=cost(64 * 10, 16 * 10**6),
        name="interior",
    )(offs, aggregate_ids, tile_values, basis_tiles)
    early_all = exchange(early)
    prol, late = pl.pallas_call(
        functools.partial(rim_kernel, rows, total),
        out_shape=[sds((rows, 3, *block), bf16), sds((4, *block), bf16)],
        in_specs=[SM, VM, VM, ANY, ANY, VM, VM, ANY],
        out_specs=[ANY, VM],
        scratch_shapes=[
            pltpu.VMEM((2, 6, 3, *block), bf16),
            pltpu.VMEM((2, 6, *block), bf16),
            pltpu.VMEM((2, 2, 3, *block), bf16),
            pltpu.VMEM((2, 10, size, 2 * width), bf16),
            DMA((6,)),
        ],
        input_output_aliases={7: 0},
        compiler_params=pltpu.CompilerParams(vmem_limit_bytes=16 * 2**20),
        cost_estimate=cost(140, 3 * 10**6),
        name="rim",
    )(offs, from_low, from_high, tile_values, basis_tiles, pc, mid, prol)
    late_all = exchange(late)
    operands = [x for pair in zip(late_all, early_all) for x in pair]
    coarse = pl.pallas_call(
        functools.partial(place_kernel, rows),
        out_shape=sds((4 * MOSTA, 3, *block), bf16),
        in_specs=[SM] + [VM] * 8,
        out_specs=VM,
        compiler_params=pltpu.CompilerParams(vmem_limit_bytes=16 * 2**20),
        cost_estimate=cost(0, 3 * 10**6),
        name="place",
    )(aggregate_ids, *operands)
    return prol, coarse


def solution(mesh):
    placed = (P(AXES, None, None, None), P(AXES, None, None), P(), P())
    return jax.shard_map(
        local,
        mesh=mesh,
        in_specs=placed,
        out_specs=(P(AXES, None, None, None), P("dev", None, None, None)),
        check_vma=False,
    )
```

```python
import functools

import jax
import jax.numpy as jnp
from jax import lax
from jax.experimental import pallas as pl
from jax.experimental.pallas import tpu as pltpu
from jax.sharding import PartitionSpec as P

MOSTA = 4
GRP = 8
HALF = 4
damping = 0.6
f32, bf16 = jnp.float32, jnp.bfloat16
AXES = ("region", "dev")
LIMITS = (16.0, 40.0, 16.0)


def row_scale(diagonal_tile):
    size = diagonal_tile.shape[0]
    on = lax.broadcasted_iota(jnp.int32, (size, size), 0) == lax.broadcasted_iota(
        jnp.int32, (size, size), 1
    )
    kept = jnp.where(on, diagonal_tile, jnp.zeros_like(diagonal_tile))
    diag = dot(kept, jnp.ones_like(kept))
    return -damping * (1.0 / jnp.where(diag == 0.0, 1.0, diag))


def dot(a, b):
    return jnp.dot(a, b, preferred_element_type=f32)


def dot_t(a, b):
    return lax.dot_general(a, b, (((0,), (0,)), ((), ())), preferred_element_type=f32)


def tall(blocks):
    return jnp.concatenate(blocks, axis=0)


def wide(blocks):
    return jnp.concatenate(blocks, axis=1)


def smooth_row(tiles, near):
    scale = row_scale(tiles[0])
    head = near[0].astype(f32) + scale * dot(tiles[0], near[0])
    rest = [scale * dot(tiles[k], near[k]) for k in (1, 2)]
    return [x.astype(bf16) for x in (head, *rest)]


def place_of(rows):
    return (lax.axis_index("region") * lax.axis_size("dev") + lax.axis_index("dev")) * rows


def offsets_copy(own, total, offs_hbm, offs, sem):
    start = pl.multiple_of(jnp.clip((own - 2) // 128 * 128, 0, total - 256), 128)
    return start, pltpu.make_async_copy(offs_hbm.at[:, pl.ds(start, 256)], offs, sem)


def edges_kernel(
    rows, total, offs_hbm, tiles_hbm, basis_hbm, low_ref, high_ref, keep_ref, offs, basis, sems
):
    own = place_of(rows)
    start, offs_in = offsets_copy(own, total, offs_hbm, offs, sems.at[6])
    copies = []
    for side, out in enumerate((low_ref, high_ref)):
        outer, inner, far = (0, 2, 0) if side == 0 else (rows - 2, rows - 4, rows - 6)
        copies.append(
            [
                pltpu.make_async_copy(basis_hbm.at[pl.ds(far, 6)], basis.at[side], sems.at[3 * side]),
                pltpu.make_async_copy(tiles_hbm.at[pl.ds(outer, 2)], out.at[pl.ds(0, 2)], sems.at[3 * side + 1]),
                pltpu.make_async_copy(
                    tiles_hbm.at[pl.ds(inner, 2)], keep_ref.at[side, pl.ds(0, 2)], sems.at[3 * side + 2]
                ),
            ]
        )
    offs_in.start()
    for group in copies:
        for c in group:
            c.start()
    offs_in.wait()
    for side, out in enumerate((low_ref, high_ref)):
        for c in copies[side]:
            c.wait()
        for i in range(4):
            m = i if side == 0 else rows - 4 + i
            at = i if side == 0 else i + 2
            outer = (i < 2) == (side == 0)
            held = out.at[i % 2] if outer else keep_ref.at[side, i % 2]
            near, weights = [basis[side, at]], []
            for k in range(2):
                n = at + offs[k, own - start + m]
                weights.append(jnp.where((n >= 0) & (n <= 5), 1.0, 0.0).astype(f32))
                near.append(basis[side, jnp.clip(n, 0, 5)])
            p0, p1, p2 = smooth_row([held[k] for k in range(3)], near)
            sum_ = p0.astype(f32) + weights[0] * p1.astype(f32) + weights[1] * p2.astype(f32)
            out[2 + i // 3, i % 3] = sum_.astype(bf16)
        for i in range(2):
            out[3, 1 + i] = basis[side, i if side == 0 else 4 + i]
            keep_ref[side, 2, i] = basis[side, 2 + i]
        keep_ref[side, 2, 2] = jnp.zeros(basis.shape[2:], bf16)


def interior_kernel(
    rows, total, offs_hbm, aggs_hbm, tiles_hbm, basis_hbm, prol_hbm, early_ref, mid_ref, pc_ref,
    offs, aggs, tiles, basis, prol, cols, acc, tile_sems, basis_sems, out_sems, small_sems,
):
    own = place_of(rows)
    units = rows // GRP
    start, offs_in = offsets_copy(own, total, offs_hbm, offs, small_sems.at[0])
    aggs_in = pltpu.make_async_copy(aggs_hbm, aggs, small_sems.at[1])

    def part_of(u):
        return pl.ds(u * GRP, GRP)

    def tile_copy(u):
        return pltpu.make_async_copy(tiles_hbm.at[part_of(u)], tiles.at[part_of(u)], tile_sems.at[u])

    def basis_copy(u):
        return pltpu.make_async_copy(basis_hbm.at[part_of(u)], basis.at[part_of(u)], basis_sems.at[u])

    def out_copy(u):
        return pltpu.make_async_copy(prol.at[part_of(u)], prol_hbm.at[part_of(u)], out_sems.at[u])

    offs_in.start()
    aggs_in.start()
    basis_copy(0).start()
    for u in range(units):
        tile_copy(u).start()
        if u < units - 1:
            basis_copy(u + 1).start()
    acc[...] = jnp.zeros_like(acc)
    offs_in.wait()
    aggs_in.wait()
    basis_copy(0).wait()
    base = aggs[own]
    count = aggs[own + rows - 1] - base + 1

    def agg_of(m):
        return aggs[own + m]

    def near_of(m):
        return [m] + [jnp.clip(m + offs[k, own - start + m], 0, rows - 1) for k in range(2)]

    def smooth(u):
        mine = agg_of(u * GRP)
        slot = lax.rem(mine, 2)
        for i in range(GRP):
            m = u * GRP + i
            n = near_of(m)
            row = smooth_row([tiles[m, k] for k in range(3)], [basis[x] for x in n])
            for k in range(3):
                prol[m, k] = row[k]
            p0, p1, p2 = [x.astype(f32) for x in row]
            if 2 <= i < GRP - 2:
                cols[m, slot] = (p0 + p1 + p2).astype(bf16)
                cols[m, 1 - slot] = jnp.zeros_like(row[0])
            else:
                w1, w2 = [jnp.where(agg_of(x) == mine, 1.0, 0.0).astype(f32) for x in n[1:]]
                cols[m, slot] = (p0 + w1 * p1 + w2 * p2).astype(bf16)
                cols[m, 1 - slot] = ((1.0 - w1) * p1 + (1.0 - w2) * p2).astype(bf16)

    def window(w, columns_of):
        left, right = [], []
        for i in range(GRP):
            m = w * GRP - HALF + i
            lhs = wide([tiles[m, k] for k in range(3)])
            right.append(dot(lhs, tall([columns_of(x) for x in near_of(m)])).astype(bf16))
            left.append(columns_of(m))
        return dot_t(tall(left), tall(right))

    def step(w, u):
        low, high = agg_of((w - 1) * GRP), agg_of(w * GRP)

        @pl.when(low == high)
        def _():
            slot = lax.rem(low, 2)
            added = window(w, lambda x: cols[x, slot])
            if u is not None:
                smooth(u)
            acc[low - base, 1] += added

        @pl.when(low != high)
        def _():
            size = tiles.shape[-1]
            added = window(w, lambda x: wide([cols[x, 0], cols[x, 1]]))
            if u is not None:
                smooth(u)
            at = [jnp.where(lax.rem(low, 2) == s, low, high) for s in range(2)]
            for r in range(2):
                for s in range(2):
                    acc[at[r] - base, at[s] - at[r] + 1] += added[
                        r * size : (r + 1) * size, s * size : (s + 1) * size
                    ]

    def arrived(u):
        tile_copy(u).wait()

        @pl.when(u < units - 1)
        def _():
            basis_copy(u + 1).wait()

    for u in range(2):
        arrived(u)
        smooth(u)
        out_copy(u).start()

    def unit(u, carry):
        arrived(u)
        step(u - 1, u)
        out_copy(u).start()
        return carry

    lax.fori_loop(2, units, unit, 0)
    step(units - 1, None)
    first_slot, last_slot = lax.rem(base, 2), lax.rem(agg_of(rows - 1), 2)
    for i in range(4):
        pc_ref[i] = cols[2 + i, first_slot]
        pc_ref[4 + i] = cols[rows - 6 + i, last_slot]
    early_ref[0] = acc[0, 2].astype(bf16)
    early_ref[7] = acc[count - 1, 0].astype(bf16)
    for j in (1, 2):
        kept = jnp.where(j < count - 1, 1.0, 0.0).astype(f32)
        for b in range(3):
            early_ref[3 * j - 2 + b] = (kept * acc[j, b]).astype(bf16)
    mid_ref[0] = acc[0, 1]
    mid_ref[1] = acc[count - 1, 1]
    for u in range(units):
        out_copy(u).wait()


def rim_kernel(
    rows, total, offs_hbm, low_got, high_got, low_own, high_own, keep_ref, pc_ref, mid_ref, prol_in,
    prol_hbm, late_ref, offs, prol, cols, sems,
):
    own = place_of(rows)
    size = cols.shape[-2]
    start, offs_in = offsets_copy(own, total, offs_hbm, offs, sems.at[2])
    offs_in.start()
    offs_in.wait()
    outs = []
    for side, (got, sent) in enumerate(((low_got, low_own), (high_got, high_own))):
        first = -2 if side == 0 else rows - 4
        theirs, mine, plain = ((0, 1), (2, 3), (4, 5)) if side == 0 else ((4, 5), (2, 3), (0, 1))
        nb, me = (0, 1) if side == 0 else (1, 0)
        zero = jnp.zeros((size, size), bf16)
        basis = [None] * 6
        held = [None] * 6
        for i in range(2):
            held[theirs[i]], held[mine[i]], held[plain[i]] = got.at[i], sent.at[i], keep_ref.at[side, i]

        def basis_of(x):
            order = (got, sent, None) if side == 0 else (None, sent, got)
            where = jnp.clip(x, 0, 5)
            out = None
            for group, source in enumerate(order):
                block = (
                    keep_ref[side, 2, lax.rem(where, 2)] if source is None else source[3, 1 + lax.rem(where, 2)]
                )
                out = block if out is None else jnp.where(where // 2 == group, block, out)
            return out

        def near_of(e):
            m = own + first + e
            inside = (m >= 0) & (m < total)
            at = jnp.clip(m, 0, total - 1) - start
            return [e] + [e + jnp.where(inside, offs[k, at], 0) for k in range(2)]

        def is_mine(e):
            return (e >= 2) if side == 0 else (e <= 3)

        def put(e, which, block):
            cols[side, 2 + e, :, which * size : (which + 1) * size] = block

        for i in range(4):
            e = i - 2 if side == 0 else i + 4
            put(e, nb, got[2 + i // 3, i % 3])
            if e not in theirs:
                put(e, me, zero)
            e = i + 4 if side == 0 else i - 2
            put(e, me, pc_ref[4 * side + i])
            put(e, nb, zero)
        for e in (*mine, *theirs):
            n = near_of(e)
            row = smooth_row([held[e][k] for k in range(3)], [basis_of(x) for x in n])
            p0, p1, p2 = [x.astype(f32) for x in row]
            w1, w2 = [jnp.where(is_mine(x), 1.0, 0.0).astype(f32) for x in n[1:]]
            if e in mine:
                for k in range(3):
                    prol[side, e - 2, k] = row[k]
                put(e, me, (p0 + w1 * p1 + w2 * p2).astype(bf16))
                put(e, nb, ((1.0 - w1) * p1 + (1.0 - w2) * p2).astype(bf16))
            else:
                put(e, me, (w1 * p1 + w2 * p2).astype(bf16))
        out = pltpu.make_async_copy(
            prol.at[side], prol_hbm.at[pl.ds(0 if side == 0 else rows - 2, 2)], sems.at[side]
        )
        out.start()
        outs.append(out)
        left, right = [], []
        for e in range(6):
            n = near_of(e)
            lhs = wide([held[e][k] for k in range(3)])
            right.append(dot(lhs, tall([cols[side, 2 + x] for x in n])).astype(bf16))
            left.append(cols[side, 2 + e, :, me * size : (me + 1) * size])
        added = dot_t(tall(left), tall(right))
        if side == 0:
            late_ref[0] = added[:, :size].astype(bf16)
            late_ref[1] = (added[:, size:] + mid_ref[0]).astype(bf16)
        else:
            late_ref[2] = (added[:, :size] + mid_ref[1]).astype(bf16)
            late_ref[3] = added[:, size:].astype(bf16)
    for out in outs:
        out.wait()


def source_of(rows, j, aggs):
    source = lax.bitwise_xor(lax.axis_index("region"), j)
    own = (source * lax.axis_size("dev") + lax.axis_index("dev")) * rows
    return source * MOSTA, aggs[own + rows - 1] - aggs[own] + 1


def early_kernel(rows, aggs_hbm, *refs):
    out, aggs, sem = refs[-3:]
    aggs_in = pltpu.make_async_copy(aggs_hbm, aggs, sem)
    aggs_in.start()
    aggs_in.wait()
    for j in range(4):
        early = refs[j]
        at, count = source_of(rows, j, aggs)
        out[at, 2] = early[0]
        for b in range(3):
            out[at + 1, b] = early[1 + b]
            out[at + 2, b] = early[4 + b]
            out[at + 3, b] = jnp.zeros_like(early[0])
        out[at + count - 1, 0] = early[7]


def late_kernel(rows, aggs_hbm, *refs):
    coarse_in, out, aggs, sem, sems = refs[-5:]
    aggs_in = pltpu.make_async_copy(aggs_hbm, aggs, sem)
    aggs_in.start()
    aggs_in.wait()
    copies = []
    for j in range(4):
        late = refs[j]
        at, count = source_of(rows, j, aggs)
        copies.append(
            pltpu.make_async_copy(late.at[pl.ds(0, 2)], out.at[at, pl.ds(0, 2)], sems.at[2 * j])
        )
        copies.append(
            pltpu.make_async_copy(
                late.at[pl.ds(2, 2)], out.at[at + count - 1, pl.ds(1, 2)], sems.at[2 * j + 1]
            )
        )
    for c in copies:
        c.start()
    for c in copies:
        c.wait()


VM = pl.BlockSpec(memory_space=pltpu.VMEM)
ANY = pl.BlockSpec(memory_space=pl.ANY)
DMA = pltpu.SemaphoreType.DMA


def cost(products, bytes_accessed):
    return pl.CostEstimate(flops=2 * 128**3 * products, bytes_accessed=bytes_accessed, transcendentals=0)


def swap(block, by):
    return lax.ppermute(block, "region", [(i, i ^ by) for i in range(lax.axis_size("region"))])


def local(tile_values, basis_tiles, tile_offsets, aggregate_ids):
    rows, _, size, width = tile_values.shape
    total = tile_offsets.shape[0]
    hbm = lambda x: pltpu.with_memory_space_constraint(x, pltpu.HBM)
    tile_values, basis_tiles, aggregate_ids = hbm(tile_values), hbm(basis_tiles), hbm(aggregate_ids)
    offs_all = hbm(tile_offsets.T)
    block = (size, width)
    sds = jax.ShapeDtypeStruct
    window = pltpu.SMEM((2, 256), jnp.int32)
    ids = pltpu.SMEM((total,), jnp.int32)
    first, middle, last = [pltpu.CompilerParams(vmem_limit_bytes=int(x * 2**20)) for x in LIMITS]
    low, high, keep = pl.pallas_call(
        functools.partial(edges_kernel, rows, total),
        out_shape=[pltpu.VMEM((4, 3, *block), bf16)] * 2 + [pltpu.VMEM((2, 3, 3, *block), bf16)],
        in_specs=[ANY, ANY, ANY],
        out_specs=[VM, VM, VM],
        scratch_shapes=[window, pltpu.VMEM((2, 6, *block), bf16), DMA((7,))],
        compiler_params=first,
        cost_estimate=cost(24, 2 * 10**6),
        name="edges",
    )(offs_all, tile_values, basis_tiles)
    devices = lax.axis_size(AXES)
    from_low = lax.ppermute(high, AXES, [(i, i + 1) for i in range(devices - 1)])
    from_high = lax.ppermute(low, AXES, [(i + 1, i) for i in range(devices - 1)])
    prol, early, mid, pc = pl.pallas_call(
        functools.partial(interior_kernel, rows, total),
        out_shape=[
            sds((rows, 3, *block), bf16),
            pltpu.VMEM((8, *block), bf16),
            pltpu.VMEM((2, *block), f32),
            pltpu.VMEM((8, *block), bf16),
        ],
        in_specs=[ANY, ANY, ANY, ANY],
        out_specs=[ANY, VM, VM, VM],
        scratch_shapes=[
            window,
            ids,
            pltpu.VMEM((rows, 3, *block), bf16),
            pltpu.VMEM((rows, *block), bf16),
            pltpu.VMEM((rows, 3, *block), bf16),
            pltpu.VMEM((rows, 2, *block), bf16),
            pltpu.VMEM((MOSTA, 3, *block), f32),
            DMA((rows // GRP,)),
            DMA((rows // GRP,)),
            DMA((rows // GRP,)),
            DMA((2,)),
        ],
        compiler_params=middle,
        cost_estimate=cost(64 * 10, 16 * 10**6),
        name="interior",
    )(offs_all, aggregate_ids, tile_values, basis_tiles)
    early_across, early_beside = swap(early, 2), swap(early, 1)
    prol, late = pl.pallas_call(
        functools.partial(rim_kernel, rows, total),
        out_shape=[sds((rows, 3, *block), bf16), pltpu.VMEM((4, *block), bf16)],
        in_specs=[ANY] + [VM] * 7 + [ANY],
        out_specs=[ANY, VM],
        scratch_shapes=[
            window,
            pltpu.VMEM((2, 2, 3, *block), bf16),
            pltpu.VMEM((2, 10, size, 2 * width), bf16),
            DMA((3,)),
        ],
        input_output_aliases={8: 0},
        compiler_params=last,
        cost_estimate=cost(140, 3 * 10**6),
        name="rim",
    )(offs_all, from_low, from_high, low, high, keep, pc, mid, prol)
    late_across, late_beside = swap(late, 2), swap(late, 1)
    held, ignored = lax.optimization_barrier((early_across, late))
    early_both = swap(held, 1)
    coarse = pl.pallas_call(
        functools.partial(early_kernel, rows),
        out_shape=sds((4 * MOSTA, 3, *block), bf16),
        in_specs=[ANY] + [VM] * 4,
        out_specs=VM,
        scratch_shapes=[ids, DMA],
        compiler_params=last,
        cost_estimate=cost(0, 3 * 10**6),
        name="early",
    )(aggregate_ids, early, early_beside, early_across, early_both)
    held, coarse = lax.optimization_barrier((late_across, coarse))
    late_both = swap(held, 1)
    coarse = pl.pallas_call(
        functools.partial(late_kernel, rows),
        out_shape=sds((4 * MOSTA, 3, *block), bf16),
        in_specs=[ANY] + [VM] * 4 + [ANY],
        out_specs=ANY,
        scratch_shapes=[ids, DMA, DMA((8,))],
        input_output_aliases={5: 0},
        compiler_params=last,
        cost_estimate=cost(0, 10**6),
        name="late",
    )(aggregate_ids, late, late_beside, held, late_both, coarse)
    return prol, coarse


def solution(mesh):
    placed = (P(AXES, None, None, None), P(AXES, None, None), P(), P())
    return jax.shard_map(
        local,
        mesh=mesh,
        in_specs=placed,
        out_specs=(P(AXES, None, None, None), P("dev", None, None, None)),
        check_vma=False,
    )
```

```python
import functools

import jax
import jax.numpy as jnp
from jax import lax
from jax.experimental import pallas as pl
from jax.experimental.pallas import tpu as pltpu
from jax.sharding import PartitionSpec as P

MOSTA = 4
GRP = 8
HALF = 4
damping = 0.6
f32, bf16 = jnp.float32, jnp.bfloat16
AXES = ("region", "dev")
LIMITS = (16.0, 40.0, 16.0)


def row_scale(diagonal_tile):
    size = diagonal_tile.shape[0]
    on = lax.broadcasted_iota(jnp.int32, (size, size), 0) == lax.broadcasted_iota(
        jnp.int32, (size, size), 1
    )
    kept = jnp.where(on, diagonal_tile, jnp.zeros_like(diagonal_tile))
    diag = dot(kept, jnp.ones_like(kept))
    return -damping * (1.0 / jnp.where(diag == 0.0, 1.0, diag))


def dot(a, b):
    return jnp.dot(a, b, preferred_element_type=f32)


def dot_t(a, b):
    return lax.dot_general(a, b, (((0,), (0,)), ((), ())), preferred_element_type=f32)


def tall(blocks):
    return jnp.concatenate(blocks, axis=0)


def wide(blocks):
    return jnp.concatenate(blocks, axis=1)


def smooth_row(tiles, near):
    scale = row_scale(tiles[0])
    head = near[0].astype(f32) + scale * dot(tiles[0], near[0])
    rest = [scale * dot(tiles[k], near[k]) for k in (1, 2)]
    return [x.astype(bf16) for x in (head, *rest)]


def weight(condition):
    return jnp.where(condition, 1.0, 0.0).astype(f32)


def place_of(rows):
    return (lax.axis_index("region") * lax.axis_size("dev") + lax.axis_index("dev")) * rows


def offsets_copy(own, total, offs_hbm, offs, sem):
    start = pl.multiple_of(jnp.clip((own - 2) // 128 * 128, 0, total - 256), 128)
    return start, pltpu.make_async_copy(offs_hbm.at[:, pl.ds(start, 256)], offs, sem)


def edges_kernel(
    rows, total, offs_hbm, tiles_hbm, basis_hbm, low_ref, high_ref, tiles, basis, offs, cols, sems
):
    own = place_of(rows)
    start, offs_in = offsets_copy(own, total, offs_hbm, offs, sems.at[4])
    copies = []
    for side in range(2):
        first, far = (0, 0) if side == 0 else (rows - 4, rows - 6)
        copies.append(
            [
                pltpu.make_async_copy(basis_hbm.at[pl.ds(far, 6)], basis.at[side], sems.at[2 * side]),
                pltpu.make_async_copy(tiles_hbm.at[pl.ds(first, 4)], tiles.at[side], sems.at[2 * side + 1]),
            ]
        )
    offs_in.start()
    for group in copies:
        for c in group:
            c.start()
    offs_in.wait()
    for group in copies:
        for c in group:
            c.wait()
    for side, out in enumerate((low_ref, high_ref)):
        shift = 0 if side == 0 else 2
        outer = (0, 1) if side == 0 else (2, 3)
        near = [
            [i + shift + offs[k, own - start + (i if side == 0 else rows - 4 + i)] for k in range(2)]
            for i in range(4)
        ]
        for i in range(4):
            blocks = [basis[side, i + shift]] + [basis[side, jnp.clip(n, 0, 5)] for n in near[i]]
            p0, p1, p2 = smooth_row([tiles[side, i, k] for k in range(3)], blocks)
            w1, w2 = [weight((n >= 0) & (n <= 5)) for n in near[i]]
            cols[side, i] = (p0.astype(f32) + w1 * p1.astype(f32) + w2 * p2.astype(f32)).astype(bf16)
        for j, i in enumerate(outer):
            out[3 * j] = tiles[side, i, 0]
            for k in range(2):
                n = near[i][k]
                beyond = (n >= 2) if side == 0 else (n <= 3)
                product = dot(tiles[side, i, 1 + k], cols[side, jnp.clip(n - shift, 0, 3)]).astype(bf16)
                out[3 * j + 1 + k] = jnp.where(beyond, product, tiles[side, i, 1 + k])
            out[6 + j] = cols[side, i]
            out[8 + j] = basis[side, i + shift]


def interior_kernel(
    rows, total, offs_hbm, aggs_hbm, tiles_hbm, basis_hbm, prol_hbm, early_ref, mid_ref, pc_ref,
    offs, aggs, tiles, basis, prol, cols, acc, tile_sems, basis_sems, out_sems, small_sems,
):
    own = place_of(rows)
    units = rows // GRP
    start, offs_in = offsets_copy(own, total, offs_hbm, offs, small_sems.at[0])
    aggs_in = pltpu.make_async_copy(aggs_hbm, aggs, small_sems.at[1])

    def part_of(u):
        return pl.ds(u * GRP, GRP)

    def tile_copy(u):
        return pltpu.make_async_copy(tiles_hbm.at[part_of(u)], tiles.at[part_of(u)], tile_sems.at[u])

    def basis_copy(u):
        return pltpu.make_async_copy(basis_hbm.at[part_of(u)], basis.at[part_of(u)], basis_sems.at[u])

    def out_copy(u):
        return pltpu.make_async_copy(prol.at[part_of(u)], prol_hbm.at[part_of(u)], out_sems.at[u])

    offs_in.start()
    aggs_in.start()
    basis_copy(0).start()
    for u in range(units):
        tile_copy(u).start()
        if u < units - 1:
            basis_copy(u + 1).start()
    acc[...] = jnp.zeros_like(acc)
    offs_in.wait()
    aggs_in.wait()
    basis_copy(0).wait()
    base = aggs[own]
    count = aggs[own + rows - 1] - base + 1

    def agg_of(m):
        return aggs[own + m]

    def near_of(m):
        return [m] + [jnp.clip(m + offs[k, own - start + m], 0, rows - 1) for k in range(2)]

    def smooth(u):
        mine = agg_of(u * GRP)
        slot = lax.rem(mine, 2)
        for i in range(GRP):
            m = u * GRP + i
            n = near_of(m)
            row = smooth_row([tiles[m, k] for k in range(3)], [basis[x] for x in n])
            for k in range(3):
                prol[m, k] = row[k]
            p0, p1, p2 = [x.astype(f32) for x in row]
            if 2 <= i < GRP - 2:
                cols[m, slot] = (p0 + p1 + p2).astype(bf16)
                cols[m, 1 - slot] = jnp.zeros_like(row[0])
            else:
                w1, w2 = [jnp.where(agg_of(x) == mine, 1.0, 0.0).astype(f32) for x in n[1:]]
                cols[m, slot] = (p0 + w1 * p1 + w2 * p2).astype(bf16)
                cols[m, 1 - slot] = ((1.0 - w1) * p1 + (1.0 - w2) * p2).astype(bf16)

    def window(w, columns_of):
        left, right = [], []
        for i in range(GRP):
            m = w * GRP - HALF + i
            lhs = wide([tiles[m, k] for k in range(3)])
            right.append(dot(lhs, tall([columns_of(x) for x in near_of(m)])).astype(bf16))
            left.append(columns_of(m))
        return dot_t(tall(left), tall(right))

    def step(w, u):
        low, high = agg_of((w - 1) * GRP), agg_of(w * GRP)

        @pl.when(low == high)
        def _():
            slot = lax.rem(low, 2)
            added = window(w, lambda x: cols[x, slot])
            if u is not None:
                smooth(u)
            acc[low - base, 1] += added

        @pl.when(low != high)
        def _():
            size = tiles.shape[-1]
            added = window(w, lambda x: wide([cols[x, 0], cols[x, 1]]))
            if u is not None:
                smooth(u)
            at = [jnp.where(lax.rem(low, 2) == s, low, high) for s in range(2)]
            for r in range(2):
                for s in range(2):
                    acc[at[r] - base, at[s] - at[r] + 1] += added[
                        r * size : (r + 1) * size, s * size : (s + 1) * size
                    ]

    def arrived(u):
        tile_copy(u).wait()

        @pl.when(u < units - 1)
        def _():
            basis_copy(u + 1).wait()

    for u in range(2):
        arrived(u)
        smooth(u)
        out_copy(u).start()

    def unit(u, carry):
        arrived(u)
        step(u - 1, u)
        out_copy(u).start()
        return carry

    lax.fori_loop(2, units, unit, 0)
    step(units - 1, None)
    first_slot, last_slot = lax.rem(base, 2), lax.rem(agg_of(rows - 1), 2)
    for i in range(4):
        pc_ref[i] = cols[2 + i, first_slot]
        pc_ref[4 + i] = cols[rows - 6 + i, last_slot]
    early_ref[0] = acc[0, 2].astype(bf16)
    early_ref[7] = acc[count - 1, 0].astype(bf16)
    for j in (1, 2):
        kept = jnp.where(j < count - 1, 1.0, 0.0).astype(f32)
        for b in range(3):
            early_ref[3 * j - 2 + b] = (kept * acc[j, b]).astype(bf16)
    mid_ref[0] = acc[0, 1]
    mid_ref[1] = acc[count - 1, 1]
    for u in range(units):
        out_copy(u).wait()


def rim_kernel(
    rows, total, offs_hbm, low_got, high_got, tiles, basis, pc_ref, mid_ref, prol_in,
    prol_hbm, late_ref, offs, prol, low_cols, high_cols, sems,
):
    own = place_of(rows)
    size = low_cols.shape[-2]
    start, offs_in = offsets_copy(own, total, offs_hbm, offs, sems.at[2])
    offs_in.start()
    sides = ((0, low_got, low_cols, -2, (0, 1), (2, 3)), (1, high_got, high_cols, rows - 4, (4, 5), (2, 3)))
    scales = []
    for side, got, cols, first, theirs, mine in sides:
        own_at = (0, 1) if side == 0 else (2, 3)
        scales.append({e: row_scale(got[3 * i]) for i, e in enumerate(theirs)})
        scales[side].update({e: row_scale(tiles[side, own_at[i], 0]) for i, e in enumerate(mine)})
    offs_in.wait()

    outs, near = [], []
    for side, got, cols, first, theirs, mine in sides:
        nb, me = (0, 1) if side == 0 else (1, 0)
        shift = -2 if side == 0 else 0

        def near_of(e, first=first):
            m = own + first + e
            inside = (m >= 0) & (m < total)
            at = jnp.clip(m, 0, total - 1) - start
            return [e + jnp.where(inside, offs[k, at], 0) for k in range(2)]

        def put(e, which, block, cols=cols):
            cols[2 + e, :, which * size : (which + 1) * size] = block

        near.append([near_of(e) for e in range(6)])
        for i in range(2):
            put(theirs[i], nb, got[6 + i])
        for i in range(4):
            e = i + 4 if side == 0 else i - 2
            put(e, me, pc_ref[4 * side + i])
            put(e, nb, jnp.zeros((size, size), bf16))

        def basis_of(x, side=side, got=got, theirs=theirs):
            outside = (x < 2) if side == 0 else (x > 3)
            at = jnp.clip(x - 2 if side == 0 else x + 2, 0, 5)
            return jnp.where(outside, got[8 + lax.rem(jnp.clip(x, 0, 5), 2)], basis[side, at])

        for e in (*mine, *theirs):
            w1, w2 = [weight((x >= 2) if side == 0 else (x <= 3)) for x in near[side][e]]
            held = [got[3 * theirs.index(e) + k] if e in theirs else tiles[side, e + shift, k] for k in range(3)]
            scale = scales[side][e]
            p1, p2 = [
                (scale * dot(held[1 + k], basis_of(near[side][e][k]))).astype(bf16) for k in range(2)
            ]
            q1, q2 = p1.astype(f32), p2.astype(f32)
            if e in mine:
                here = basis[side, e - 2 if side == 0 else e + 2]
                p0 = (here.astype(f32) + scale * dot(held[0], here)).astype(bf16)
                for k, block in enumerate((p0, p1, p2)):
                    prol[side, e - 2, k] = block
                put(e, me, (p0.astype(f32) + w1 * q1 + w2 * q2).astype(bf16))
                put(e, nb, ((1.0 - w1) * q1 + (1.0 - w2) * q2).astype(bf16))
            else:
                put(e, me, (w1 * q1 + w2 * q2).astype(bf16))
    for side in range(2):
        out = pltpu.make_async_copy(
            prol.at[side], prol_hbm.at[pl.ds(0 if side == 0 else rows - 2, 2)], sems.at[side]
        )
        out.start()
        outs.append(out)
    for side, got, cols, first, theirs, mine in sides:
        nb, me = (0, 1) if side == 0 else (1, 0)
        shift = -2 if side == 0 else 0
        left, right = [], []
        for e in range(6):
            x1, x2 = near[side][e]
            if e in theirs:
                held = [got[3 * theirs.index(e) + k] for k in range(3)]
                kept = [(x >= 0) & (x <= 5) for x in (x1, x2)]
                zero = jnp.zeros_like(held[0])
                lhs = wide([held[0]] + [jnp.where(kept[k], held[1 + k], zero) for k in range(2)])
                more = sum(jnp.where(kept[k], zero, held[1 + k]).astype(f32) for k in range(2))
                x1, x2 = jnp.clip(x1, 0, 5), jnp.clip(x2, 0, 5)
            else:
                lhs, more = wide([tiles[side, e + shift, k] for k in range(3)]), None
            product = dot(lhs, tall([cols[2 + x] for x in (e, x1, x2)]))
            if more is not None:
                halves = [product[:, :size], product[:, size:]]
                halves[nb] += more
                product = wide(halves)
            right.append(product.astype(bf16))
            left.append(cols[2 + e, :, me * size : (me + 1) * size])
        added = dot_t(tall(left), tall(right))
        if side == 0:
            late_ref[0] = added[:, :size].astype(bf16)
            late_ref[1] = (added[:, size:] + mid_ref[0]).astype(bf16)
        else:
            late_ref[2] = (added[:, :size] + mid_ref[1]).astype(bf16)
            late_ref[3] = added[:, size:].astype(bf16)
    for out in outs:
        out.wait()


def place_early(block, early, count):
    block[0, 2] = early[0]
    for b in range(3):
        block[1, b] = early[1 + b]
        block[2, b] = early[4 + b]
        block[3, b] = jnp.zeros_like(early[0])
    block[count - 1, 0] = early[7]


def near_kernel(rows, aggs_hbm, early_0, early_1, out_hbm, counts, aggs, blocks, sem, sems):
    aggs_in = pltpu.make_async_copy(aggs_hbm, aggs, sem)
    aggs_in.start()
    aggs_in.wait()
    region = lax.axis_index("region")
    copies = []
    for j in range(4):
        source = lax.bitwise_xor(region, j)
        own = (source * lax.axis_size("dev") + lax.axis_index("dev")) * rows
        count = aggs[own + rows - 1] - aggs[own] + 1
        counts[j : j + 1, :] = jnp.full((1, counts.shape[1]), count, jnp.int32)
        if j < 2:
            place_early(blocks.at[j], (early_0, early_1)[j], count)
            copies.append(
                pltpu.make_async_copy(blocks.at[j], out_hbm.at[pl.ds(source * MOSTA, MOSTA)], sems.at[j])
            )
            copies[j].start()
    for c in copies:
        c.wait()


def far_kernel(counts, early_2, early_3, late_0, late_1, late_2, late_3, coarse_in, out, blocks, sems):
    region = lax.axis_index("region")
    copies = []
    for j, late in enumerate((late_0, late_1)):
        at = lax.bitwise_xor(region, j) * MOSTA
        copies.append(pltpu.make_async_copy(late.at[pl.ds(0, 2)], out.at[at, pl.ds(0, 2)], sems.at[2 * j]))
        copies.append(
            pltpu.make_async_copy(
                late.at[pl.ds(2, 2)], out.at[at + counts[j, 0] - 1, pl.ds(1, 2)], sems.at[2 * j + 1]
            )
        )
    for c in copies:
        c.start()
    for j, (early, late) in enumerate(((early_2, late_2), (early_3, late_3))):
        block, count = blocks.at[j], counts[2 + j, 0]
        place_early(block, early, count)
        for b in range(2):
            block[0, b] = late[b]
            block[count - 1, 1 + b] = late[2 + b]
        at = lax.bitwise_xor(region, 2 + j) * MOSTA
        copies.append(pltpu.make_async_copy(block, out.at[pl.ds(at, MOSTA)], sems.at[4 + j]))
        copies[-1].start()
    for c in copies:
        c.wait()


VM = pl.BlockSpec(memory_space=pltpu.VMEM)
ANY = pl.BlockSpec(memory_space=pl.ANY)
DMA = pltpu.SemaphoreType.DMA


def cost(products, bytes_accessed):
    return pl.CostEstimate(flops=2 * 128**3 * products, bytes_accessed=bytes_accessed, transcendentals=0)


def swap(block, by):
    return lax.ppermute(block, "region", [(i, i ^ by) for i in range(lax.axis_size("region"))])


def local(tile_values, basis_tiles, tile_offsets, aggregate_ids):
    rows, _, size, width = tile_values.shape
    total = tile_offsets.shape[0]
    hbm = lambda x: pltpu.with_memory_space_constraint(x, pltpu.HBM)
    tile_values, basis_tiles, aggregate_ids = hbm(tile_values), hbm(basis_tiles), hbm(aggregate_ids)
    offs_all = hbm(tile_offsets.T)
    block = (size, width)
    sds = jax.ShapeDtypeStruct
    window = pltpu.SMEM((2, 256), jnp.int32)
    ids = pltpu.SMEM((total,), jnp.int32)
    first, middle, last = [pltpu.CompilerParams(vmem_limit_bytes=int(x * 2**20)) for x in LIMITS]
    low, high, edge_tiles, edge_basis = pl.pallas_call(
        functools.partial(edges_kernel, rows, total),
        out_shape=[pltpu.VMEM(x + block, bf16) for x in ((10,), (10,), (2, 4, 3), (2, 6))],
        in_specs=[ANY, ANY, ANY],
        out_specs=[VM] * 4,
        scratch_shapes=[window, pltpu.VMEM((2, 4, *block), bf16), DMA((5,))],
        compiler_params=first,
        cost_estimate=cost(24, 2 * 10**6),
        name="edges",
    )(offs_all, tile_values, basis_tiles)
    devices = lax.axis_size(AXES)
    from_low = lax.ppermute(high, AXES, [(i, i + 1) for i in range(devices - 1)])
    from_high = lax.ppermute(low, AXES, [(i + 1, i) for i in range(devices - 1)])
    prol, early, mid, pc = pl.pallas_call(
        functools.partial(interior_kernel, rows, total),
        out_shape=[
            sds((rows, 3, *block), bf16),
            pltpu.VMEM((8, *block), bf16),
            pltpu.VMEM((2, *block), f32),
            pltpu.VMEM((8, *block), bf16),
        ],
        in_specs=[ANY, ANY, ANY, ANY],
        out_specs=[ANY, VM, VM, VM],
        scratch_shapes=[
            window,
            ids,
            pltpu.VMEM((rows, 3, *block), bf16),
            pltpu.VMEM((rows, *block), bf16),
            pltpu.VMEM((rows, 3, *block), bf16),
            pltpu.VMEM((rows, 2, *block), bf16),
            pltpu.VMEM((MOSTA, 3, *block), f32),
            DMA((rows // GRP,)),
            DMA((rows // GRP,)),
            DMA((rows // GRP,)),
            DMA((2,)),
        ],
        compiler_params=middle,
        cost_estimate=cost(64 * 10, 16 * 10**6),
        name="interior",
    )(offs_all, aggregate_ids, tile_values, basis_tiles)
    early_across, early_beside = swap(early, 2), swap(early, 1)
    prol, late = pl.pallas_call(
        functools.partial(rim_kernel, rows, total),
        out_shape=[sds((rows, 3, *block), bf16), pltpu.VMEM((4, *block), bf16)],
        in_specs=[ANY] + [VM] * 6 + [ANY],
        out_specs=[ANY, VM],
        scratch_shapes=[
            window,
            pltpu.VMEM((2, 2, 3, *block), bf16),
            pltpu.VMEM((10, size, 2 * width), bf16),
            pltpu.VMEM((10, size, 2 * width), bf16),
            DMA((3,)),
        ],
        input_output_aliases={7: 0},
        compiler_params=last,
        cost_estimate=cost(140, 3 * 10**6),
        name="rim",
    )(offs_all, from_low, from_high, edge_tiles, edge_basis, pc, mid, prol)
    late_across, late_beside = swap(late, 2), swap(late, 1)
    coarse, counts = pl.pallas_call(
        functools.partial(near_kernel, rows),
        out_shape=[sds((4 * MOSTA, 3, *block), bf16), pltpu.VMEM((8, 128), jnp.int32)],
        in_specs=[ANY, VM, VM],
        out_specs=[ANY, VM],
        scratch_shapes=[ids, pltpu.VMEM((2, MOSTA, 3, *block), bf16), DMA, DMA((2,))],
        compiler_params=last,
        cost_estimate=cost(0, 2 * 10**6),
        name="near",
    )(aggregate_ids, early, early_beside)
    early_across, late_across, coarse = lax.optimization_barrier((early_across, late_across, coarse))
    early_both, late_both = swap(early_across, 1), swap(late_across, 1)
    coarse = pl.pallas_call(
        far_kernel,
        out_shape=sds((4 * MOSTA, 3, *block), bf16),
        in_specs=[VM] * 7 + [ANY],
        out_specs=ANY,
        scratch_shapes=[pltpu.VMEM((2, MOSTA, 3, *block), bf16), DMA((6,))],
        input_output_aliases={7: 0},
        compiler_params=last,
        cost_estimate=cost(0, 2 * 10**6),
        name="far",
    )(counts, early_across, early_both, late, late_beside, late_across, late_both, coarse)
    return prol, coarse


def solution(mesh):
    placed = (P(AXES, None, None, None), P(AXES, None, None), P(), P())
    return jax.shard_map(
        local,
        mesh=mesh,
        in_specs=placed,
        out_specs=(P(AXES, None, None, None), P("dev", None, None, None)),
        check_vma=False,
    )
```

```python
import functools

import jax
import jax.numpy as jnp
from jax import lax
from jax.experimental import pallas as pl
from jax.experimental.pallas import tpu as pltpu
from jax.sharding import PartitionSpec as P

MOSTA = 4
GRP = 8
HALF = 4
damping = 0.6
f32, bf16 = jnp.float32, jnp.bfloat16
AXES = ("region", "dev")
LIMITS = (16.0, 40.0, 16.0)


def row_scale(diagonal_tile):
    size = diagonal_tile.shape[0]
    on = lax.broadcasted_iota(jnp.int32, (size, size), 0) == lax.broadcasted_iota(
        jnp.int32, (size, size), 1
    )
    kept = jnp.where(on, diagonal_tile, jnp.zeros_like(diagonal_tile))
    diag = dot(kept, jnp.ones_like(kept))
    return -damping * (1.0 / jnp.where(diag == 0.0, 1.0, diag))


def dot(a, b):
    return jnp.dot(a, b, preferred_element_type=f32)


def dot_t(a, b):
    return lax.dot_general(a, b, (((0,), (0,)), ((), ())), preferred_element_type=f32)


def tall(blocks):
    return jnp.concatenate(blocks, axis=0)


def wide(blocks):
    return jnp.concatenate(blocks, axis=1)


def smooth_row(tiles, near):
    scale = row_scale(tiles[0])
    head = near[0].astype(f32) + scale * dot(tiles[0], near[0])
    rest = [scale * dot(tiles[k], near[k]) for k in (1, 2)]
    return [x.astype(bf16) for x in (head, *rest)]


def weight(condition):
    return jnp.where(condition, 1.0, 0.0).astype(f32)


def place_of(rows):
    return (lax.axis_index("region") * lax.axis_size("dev") + lax.axis_index("dev")) * rows


def offsets_copy(own, total, offs_hbm, offs, sem):
    start = pl.multiple_of(jnp.clip((own - 2) // 128 * 128, 0, total - 256), 128)
    return start, pltpu.make_async_copy(offs_hbm.at[:, pl.ds(start, 256)], offs, sem)


def side_of(rows, own, step):
    odd = lax.rem(own // rows, 2)
    side = 1 - odd if step == 0 else odd
    return side, 1 - 2 * side


def edges_kernel(
    rows, total, offs_hbm, tiles_hbm, basis_hbm, first_ref, second_ref, tiles, basis, offs, cols, sems
):
    own = place_of(rows)
    start, offs_in = offsets_copy(own, total, offs_hbm, offs, sems.at[4])
    copies = []
    for t in range(2):
        side, way = side_of(rows, own, t)
        copies.append(
            [
                pltpu.make_async_copy(
                    basis_hbm.at[pl.ds(side * (rows - 6), 6)], basis.at[t], sems.at[2 * t]
                ),
                pltpu.make_async_copy(
                    tiles_hbm.at[pl.ds(side * (rows - 4), 4)], tiles.at[t], sems.at[2 * t + 1]
                ),
            ]
        )
    offs_in.start()
    for group in copies:
        for c in group:
            c.start()
    offs_in.wait()
    for group in copies:
        for c in group:
            c.wait()
    for t, out in enumerate((first_ref, second_ref)):
        side, way = side_of(rows, own, t)

        def tile(d, k, t=t, side=side, way=way):
            return tiles[t, side * 3 + way * d, k]

        def block(d, t=t, side=side, way=way):
            return basis[t, side * 5 + way * d]

        near = [
            [d + way * offs[k, own - start + side * (rows - 1) + way * d] for k in range(2)] for d in range(4)
        ]
        for d in range(4):
            blocks = [block(d)] + [block(jnp.clip(n, 0, 5)) for n in near[d]]
            p0, p1, p2 = smooth_row([tile(d, k) for k in range(3)], blocks)
            w1, w2 = [weight(n >= 0) for n in near[d]]
            cols[t, d] = (p0.astype(f32) + w1 * p1.astype(f32) + w2 * p2.astype(f32)).astype(bf16)
        for d in range(2):
            out[3 * d] = tile(d, 0)
            for k in range(2):
                n = near[d][k]
                product = dot(tile(d, 1 + k), cols[t, jnp.clip(n, 0, 3)]).astype(bf16)
                out[3 * d + 1 + k] = jnp.where(n >= 2, product, tile(d, 1 + k))
            out[6 + d] = cols[t, d]
            out[8 + d] = block(d)


def interior_kernel(
    rows, total, offs_hbm, aggs_hbm, tiles_hbm, basis_hbm, prol_hbm, early_ref, mid_ref, pc_ref,
    offs, aggs, tiles, basis, prol, cols, acc, tile_sems, basis_sems, out_sems, small_sems,
):
    own = place_of(rows)
    units = rows // GRP
    start, offs_in = offsets_copy(own, total, offs_hbm, offs, small_sems.at[0])
    aggs_in = pltpu.make_async_copy(aggs_hbm, aggs, small_sems.at[1])

    def part_of(u):
        return pl.ds(u * GRP, GRP)

    def tile_copy(u):
        return pltpu.make_async_copy(tiles_hbm.at[part_of(u)], tiles.at[part_of(u)], tile_sems.at[u])

    def basis_copy(u):
        return pltpu.make_async_copy(basis_hbm.at[part_of(u)], basis.at[part_of(u)], basis_sems.at[u])

    def out_copy(u):
        return pltpu.make_async_copy(prol.at[part_of(u)], prol_hbm.at[part_of(u)], out_sems.at[u])

    offs_in.start()
    aggs_in.start()
    basis_copy(0).start()
    for u in range(units):
        tile_copy(u).start()
        if u < units - 1:
            basis_copy(u + 1).start()
    acc[...] = jnp.zeros_like(acc)
    offs_in.wait()
    aggs_in.wait()
    basis_copy(0).wait()
    base = aggs[own]
    count = aggs[own + rows - 1] - base + 1

    def agg_of(m):
        return aggs[own + m]

    def near_of(m):
        return [m] + [jnp.clip(m + offs[k, own - start + m], 0, rows - 1) for k in range(2)]

    def smooth(u):
        mine = agg_of(u * GRP)
        slot = lax.rem(mine, 2)
        for i in range(GRP):
            m = u * GRP + i
            n = near_of(m)
            row = smooth_row([tiles[m, k] for k in range(3)], [basis[x] for x in n])
            for k in range(3):
                prol[m, k] = row[k]
            p0, p1, p2 = [x.astype(f32) for x in row]
            if 2 <= i < GRP - 2:
                cols[m, slot] = (p0 + p1 + p2).astype(bf16)
                cols[m, 1 - slot] = jnp.zeros_like(row[0])
            else:
                w1, w2 = [jnp.where(agg_of(x) == mine, 1.0, 0.0).astype(f32) for x in n[1:]]
                cols[m, slot] = (p0 + w1 * p1 + w2 * p2).astype(bf16)
                cols[m, 1 - slot] = ((1.0 - w1) * p1 + (1.0 - w2) * p2).astype(bf16)

    def window(w, columns_of):
        left, right = [], []
        for i in range(GRP):
            m = w * GRP - HALF + i
            lhs = wide([tiles[m, k] for k in range(3)])
            right.append(dot(lhs, tall([columns_of(x) for x in near_of(m)])).astype(bf16))
            left.append(columns_of(m))
        return dot_t(tall(left), tall(right))

    def step(w, u):
        low, high = agg_of((w - 1) * GRP), agg_of(w * GRP)

        @pl.when(low == high)
        def _():
            slot = lax.rem(low, 2)
            added = window(w, lambda x: cols[x, slot])
            if u is not None:
                smooth(u)
            acc[low - base, 1] += added

        @pl.when(low != high)
        def _():
            size = tiles.shape[-1]
            added = window(w, lambda x: wide([cols[x, 0], cols[x, 1]]))
            if u is not None:
                smooth(u)
            at = [jnp.where(lax.rem(low, 2) == s, low, high) for s in range(2)]
            for r in range(2):
                for s in range(2):
                    acc[at[r] - base, at[s] - at[r] + 1] += added[
                        r * size : (r + 1) * size, s * size : (s + 1) * size
                    ]

    def arrived(u):
        tile_copy(u).wait()

        @pl.when(u < units - 1)
        def _():
            basis_copy(u + 1).wait()

    for u in range(2):
        arrived(u)
        smooth(u)
        out_copy(u).start()

    def unit(u, carry):
        arrived(u)
        step(u - 1, u)
        out_copy(u).start()
        return carry

    lax.fori_loop(2, units, unit, 0)
    step(units - 1, None)
    first_slot, last_slot = lax.rem(base, 2), lax.rem(agg_of(rows - 1), 2)
    for i in range(4):
        pc_ref[i] = cols[2 + i, first_slot]
        pc_ref[4 + i] = cols[rows - 6 + i, last_slot]
    early_ref[0] = acc[0, 2].astype(bf16)
    early_ref[7] = acc[count - 1, 0].astype(bf16)
    for j in (1, 2):
        kept = jnp.where(j < count - 1, 1.0, 0.0).astype(f32)
        for b in range(3):
            early_ref[3 * j - 2 + b] = (kept * acc[j, b]).astype(bf16)
    mid_ref[0] = acc[0, 1]
    mid_ref[1] = acc[count - 1, 1]
    for u in range(units):
        out_copy(u).wait()


def rim_kernel(
    rows, total, offs_hbm, first_got, second_got, tiles, basis, pc_ref, mid_ref, prol_in,
    prol_hbm, late_ref, offs, first_prol, second_prol, first_cols, second_cols, sems,
):
    own = place_of(rows)
    size = tiles.shape[-1]
    start, offs_in = offsets_copy(own, total, offs_hbm, offs, sems.at[2])
    offs_in.start()
    borders = []
    for step, got, prol, cols in ((0, first_got, first_prol, first_cols), (1, second_got, second_prol, second_cols)):
        side, way = side_of(rows, own, step)

        def tile(f, k, step=step, got=got, side=side, way=way):
            return got[3 * (1 - f) + k] if f < 2 else tiles[step, side * 3 + way * (f - 2), k]

        scales = [row_scale(tile(f, 0)) for f in range(4)]
        for f in range(2):
            cols[f, :, :size] = got[7 - f]
        for i in range(4):
            cols[4 + i, :, size:] = pc_ref[side * 7 + way * i]
            cols[4 + i, :, :size] = jnp.zeros((size, size), bf16)
        borders.append((step, got, prol, cols, side, way, tile, scales))
    offs_in.wait()

    near = []
    for step, got, prol, cols, side, way, tile, scales in borders:

        def near_of(f, side=side, way=way):
            m = own + side * (rows - 1) + way * (f - 2)
            inside = (m >= 0) & (m < total)
            at = jnp.clip(m, 0, total - 1) - start
            return [f + way * jnp.where(inside, offs[k, at], 0) for k in range(2)]

        def basis_of(x, step=step, got=got, side=side, way=way):
            mine = basis[step, side * 5 + way * jnp.clip(x - 2, 0, 5)]
            return jnp.where(x < 2, got[9 - jnp.clip(x, 0, 1)], mine)

        near.append([near_of(f) for f in range(6)])
        for f in (2, 3, 0, 1):
            w1, w2 = [weight(x >= 2) for x in near[step][f]]
            p1, p2 = [
                (scales[f] * dot(tile(f, 1 + k), basis_of(near[step][f][k]))).astype(bf16) for k in range(2)
            ]
            q1, q2 = p1.astype(f32), p2.astype(f32)
            if f >= 2:
                here = basis[step, side * 5 + way * (f - 2)]
                p0 = (here.astype(f32) + scales[f] * dot(tile(f, 0), here)).astype(bf16)
                for k, block in enumerate((p0, p1, p2)):
                    prol[side + way * (f - 2), k] = block
                cols[f, :, size:] = (p0.astype(f32) + w1 * q1 + w2 * q2).astype(bf16)
                cols[f, :, :size] = ((1.0 - w1) * q1 + (1.0 - w2) * q2).astype(bf16)
            else:
                cols[f, :, size:] = (w1 * q1 + w2 * q2).astype(bf16)
    outs = []
    for step, got, prol, cols, side, way, tile, scales in borders:
        outs.append(pltpu.make_async_copy(prol, prol_hbm.at[pl.ds(side * (rows - 2), 2)], sems.at[step]))
        outs[step].start()
    products = []
    for step, got, prol, cols, side, way, tile, scales in borders:
        left, right = [], []
        for f in range(6):
            x1, x2 = near[step][f]
            if f < 2:
                zero = jnp.zeros((size, size), bf16)
                lhs = wide([tile(f, 0)] + [jnp.where(x >= 0, tile(f, 1 + k), zero) for k, x in enumerate((x1, x2))])
                more = sum(jnp.where(x >= 0, zero, tile(f, 1 + k)).astype(f32) for k, x in enumerate((x1, x2)))
                x1, x2 = jnp.clip(x1, 0, 3), jnp.clip(x2, 0, 3)
                product = dot(lhs, tall([cols[x] for x in (f, x1, x2)]))
                product = wide([product[:, :size] + more, product[:, size:]])
            else:
                product = dot(wide([tile(f, k) for k in range(3)]), tall([cols[x] for x in (f, x1, x2)]))
            right.append(product.astype(bf16))
            left.append(cols[f, :, size:])
        products.append(dot_t(tall(left), tall(right)))
    for step, got, prol, cols, side, way, tile, scales in borders:
        late_ref[3 * side] = products[step][:, :size].astype(bf16)
        late_ref[side + 1] = (products[step][:, size:] + mid_ref[side]).astype(bf16)
    for out in outs:
        out.wait()


def place_rows(block, early, late, count):
    block[0, 0] = late[0]
    block[0, 1] = late[1]
    block[0, 2] = early[0]
    for b in range(3):
        block[1, b] = early[1 + b]
        block[2, b] = early[4 + b]
        block[3, b] = jnp.zeros_like(early[0])
    block[count - 1, 0] = early[7]
    block[count - 1, 1] = late[2]
    block[count - 1, 2] = late[3]


def near_kernel(rows, aggs_hbm, early_0, early_1, late_0, late_1, out_hbm, counts, aggs, blocks, sem, sems):
    aggs_in = pltpu.make_async_copy(aggs_hbm, aggs, sem)
    aggs_in.start()
    aggs_in.wait()
    region = lax.axis_index("region")
    copies = []
    for j in range(4):
        source = lax.bitwise_xor(region, j)
        own = (source * lax.axis_size("dev") + lax.axis_index("dev")) * rows
        count = aggs[own + rows - 1] - aggs[own] + 1
        counts[j : j + 1, :] = jnp.full((1, counts.shape[1]), count, jnp.int32)
        if j < 2:
            place_rows(blocks.at[j], (early_0, early_1)[j], (late_0, late_1)[j], count)
            copies.append(
                pltpu.make_async_copy(blocks.at[j], out_hbm.at[pl.ds(source * MOSTA, MOSTA)], sems.at[j])
            )
            copies[j].start()
    for c in copies:
        c.wait()


def far_kernel(counts, early_2, early_3, late_2, late_3, coarse_in, out, blocks, sems):
    region = lax.axis_index("region")
    copies = []
    for j, (early, late) in enumerate(((early_2, late_2), (early_3, late_3))):
        place_rows(blocks.at[j], early, late, counts[2 + j, 0])
        at = lax.bitwise_xor(region, 2 + j) * MOSTA
        copies.append(pltpu.make_async_copy(blocks.at[j], out.at[pl.ds(at, MOSTA)], sems.at[j]))
        copies[j].start()
    for c in copies:
        c.wait()


VM = pl.BlockSpec(memory_space=pltpu.VMEM)
ANY = pl.BlockSpec(memory_space=pl.ANY)
DMA = pltpu.SemaphoreType.DMA


def cost(products, bytes_accessed):
    return pl.CostEstimate(flops=2 * 128**3 * products, bytes_accessed=bytes_accessed, transcendentals=0)


def swap(block, by):
    return lax.ppermute(block, "region", [(i, i ^ by) for i in range(lax.axis_size("region"))])


def local(tile_values, basis_tiles, tile_offsets, aggregate_ids):
    rows, _, size, width = tile_values.shape
    total = tile_offsets.shape[0]
    hbm = lambda x: pltpu.with_memory_space_constraint(x, pltpu.HBM)
    tile_values, basis_tiles, aggregate_ids = hbm(tile_values), hbm(basis_tiles), hbm(aggregate_ids)
    offs_all = hbm(tile_offsets.T)
    block = (size, width)
    sds = jax.ShapeDtypeStruct
    window = pltpu.SMEM((2, 256), jnp.int32)
    ids = pltpu.SMEM((total,), jnp.int32)
    first, middle, last = [pltpu.CompilerParams(vmem_limit_bytes=int(x * 2**20)) for x in LIMITS]
    first_out, second_out, edge_tiles, edge_basis = pl.pallas_call(
        functools.partial(edges_kernel, rows, total),
        out_shape=[pltpu.VMEM(x + block, bf16) for x in ((10,), (10,), (2, 4, 3), (2, 6))],
        in_specs=[ANY, ANY, ANY],
        out_specs=[VM] * 4,
        scratch_shapes=[window, pltpu.VMEM((2, 4, *block), bf16), DMA((5,))],
        compiler_params=first,
        cost_estimate=cost(24, 2 * 10**6),
        name="edges",
    )(offs_all, tile_values, basis_tiles)
    devices = lax.axis_size(AXES)
    first_pairs = [(i, i + 1) for i in range(0, devices - 1, 2)]
    second_pairs = [(i, i + 1) for i in range(1, devices - 1, 2)]
    got = [
        lax.ppermute(x, AXES, pairs + [(j, i) for i, j in pairs])
        for x, pairs in ((first_out, first_pairs), (second_out, second_pairs))
    ]
    prol, early, mid, pc = pl.pallas_call(
        functools.partial(interior_kernel, rows, total),
        out_shape=[
            sds((rows, 3, *block), bf16),
            pltpu.VMEM((8, *block), bf16),
            pltpu.VMEM((2, *block), f32),
            pltpu.VMEM((8, *block), bf16),
        ],
        in_specs=[ANY, ANY, ANY, ANY],
        out_specs=[ANY, VM, VM, VM],
        scratch_shapes=[
            window,
            ids,
            pltpu.VMEM((rows, 3, *block), bf16),
            pltpu.VMEM((rows, *block), bf16),
            pltpu.VMEM((rows, 3, *block), bf16),
            pltpu.VMEM((rows, 2, *block), bf16),
            pltpu.VMEM((MOSTA, 3, *block), f32),
            DMA((rows // GRP,)),
            DMA((rows // GRP,)),
            DMA((rows // GRP,)),
            DMA((2,)),
        ],
        compiler_params=middle,
        cost_estimate=cost(64 * 10, 16 * 10**6),
        name="interior",
    )(offs_all, aggregate_ids, tile_values, basis_tiles)
    early_across, early_beside = swap(early, 2), swap(early, 1)
    prol, late = pl.pallas_call(
        functools.partial(rim_kernel, rows, total),
        out_shape=[sds((rows, 3, *block), bf16), pltpu.VMEM((4, *block), bf16)],
        in_specs=[ANY] + [VM] * 6 + [ANY],
        out_specs=[ANY, VM],
        scratch_shapes=[
            window,
            pltpu.VMEM((2, 3, *block), bf16),
            pltpu.VMEM((2, 3, *block), bf16),
            pltpu.VMEM((8, size, 2 * width), bf16),
            pltpu.VMEM((8, size, 2 * width), bf16),
            DMA((3,)),
        ],
        input_output_aliases={7: 0},
        compiler_params=last,
        cost_estimate=cost(140, 2 * 10**6),
        name="rim",
    )(offs_all, *got, edge_tiles, edge_basis, pc, mid, prol)
    late_across, late_beside = swap(late, 2), swap(late, 1)
    coarse, counts = pl.pallas_call(
        functools.partial(near_kernel, rows),
        out_shape=[sds((4 * MOSTA, 3, *block), bf16), pltpu.VMEM((8, 128), jnp.int32)],
        in_specs=[ANY] + [VM] * 4,
        out_specs=[ANY, VM],
        scratch_shapes=[ids, pltpu.VMEM((2, MOSTA, 3, *block), bf16), DMA, DMA((2,))],
        compiler_params=last,
        cost_estimate=cost(0, 2 * 10**6),
        name="near",
    )(aggregate_ids, early, early_beside, late, late_beside)
    early_across, late_across, coarse = lax.optimization_barrier((early_across, late_across, coarse))
    early_both, late_both = swap(early_across, 1), swap(late_across, 1)
    coarse = pl.pallas_call(
        far_kernel,
        out_shape=sds((4 * MOSTA, 3, *block), bf16),
        in_specs=[VM] * 5 + [ANY],
        out_specs=ANY,
        scratch_shapes=[pltpu.VMEM((2, MOSTA, 3, *block), bf16), DMA((2,))],
        input_output_aliases={5: 0},
        compiler_params=last,
        cost_estimate=cost(0, 2 * 10**6),
        name="far",
    )(counts, early_across, early_both, late_across, late_both, coarse)
    return prol, coarse


def solution(mesh):
    placed = (P(AXES, None, None, None), P(AXES, None, None), P(), P())
    return jax.shard_map(
        local,
        mesh=mesh,
        in_specs=placed,
        out_specs=(P(AXES, None, None, None), P("dev", None, None, None)),
        check_vma=False,
    )
```

```python
import functools

import jax
import jax.numpy as jnp
from jax import lax
from jax.experimental import pallas as pl
from jax.experimental.pallas import tpu as pltpu
from jax.sharding import PartitionSpec as P

MOSTA = 4
GRP = 8
HALF = 4
damping = 0.6
f32, bf16 = jnp.float32, jnp.bfloat16
AXES = ("region", "dev")
LIMITS = (16.0, 40.0, 16.0)


def row_scale(diagonal_tile):
    size = diagonal_tile.shape[0]
    on = lax.broadcasted_iota(jnp.int32, (size, size), 0) == lax.broadcasted_iota(
        jnp.int32, (size, size), 1
    )
    diag = jnp.sum(jnp.where(on, diagonal_tile.astype(f32), 0.0), axis=1, keepdims=True)
    return -damping * (1.0 / jnp.where(diag == 0.0, 1.0, diag))


def dot(a, b):
    return jnp.dot(a, b, preferred_element_type=f32)


def dot_t(a, b):
    return lax.dot_general(a, b, (((0,), (0,)), ((), ())), preferred_element_type=f32)


def tall(blocks):
    return jnp.concatenate(blocks, axis=0)


def wide(blocks):
    return jnp.concatenate(blocks, axis=1)


def smooth_row(tiles, near):
    scale = row_scale(tiles[0])
    head = near[0].astype(f32) + scale * dot(tiles[0], near[0])
    rest = [scale * dot(tiles[k], near[k]) for k in (1, 2)]
    return [x.astype(bf16) for x in (head, *rest)]


def weight(condition):
    return jnp.where(condition, 1.0, 0.0).astype(f32)


def place_of(rows):
    return (lax.axis_index("region") * lax.axis_size("dev") + lax.axis_index("dev")) * rows


def offsets_copy(own, total, offs_hbm, offs, sem):
    start = pl.multiple_of(jnp.clip((own - 2) // 128 * 128, 0, total - 256), 128)
    return start, pltpu.make_async_copy(offs_hbm.at[:, pl.ds(start, 256)], offs, sem)


def side_of(rows, own, step):
    odd = lax.rem(own // rows, 2)
    side = 1 - odd if step == 0 else odd
    return side, 1 - 2 * side


def edges_kernel(
    rows, total, offs_hbm, tiles_hbm, basis_hbm, first_ref, second_ref, tiles, basis, offs, cols, sems
):
    own = place_of(rows)
    start, offs_in = offsets_copy(own, total, offs_hbm, offs, sems.at[4])
    copies = []
    for t in range(2):
        side, way = side_of(rows, own, t)
        copies.append(
            [
                pltpu.make_async_copy(
                    basis_hbm.at[pl.ds(side * (rows - 6), 6)], basis.at[t], sems.at[2 * t]
                ),
                pltpu.make_async_copy(
                    tiles_hbm.at[pl.ds(side * (rows - 4), 4)], tiles.at[t], sems.at[2 * t + 1]
                ),
            ]
        )
    offs_in.start()
    for group in copies:
        for c in group:
            c.start()
    offs_in.wait()
    for group in copies:
        for c in group:
            c.wait()
    for t, out in enumerate((first_ref, second_ref)):
        side, way = side_of(rows, own, t)

        def tile(d, k, t=t, side=side, way=way):
            return tiles[t, side * 3 + way * d, k]

        def block(d, t=t, side=side, way=way):
            return basis[t, side * 5 + way * d]

        near = [
            [d + way * offs[k, own - start + side * (rows - 1) + way * d] for k in range(2)] for d in range(4)
        ]
        for d in range(4):
            blocks = [block(d)] + [block(jnp.clip(n, 0, 5)) for n in near[d]]
            p0, p1, p2 = smooth_row([tile(d, k) for k in range(3)], blocks)
            w1, w2 = [weight(n >= 0) for n in near[d]]
            cols[t, d] = (p0.astype(f32) + w1 * p1.astype(f32) + w2 * p2.astype(f32)).astype(bf16)
        for d in range(2):
            out[3 * d] = tile(d, 0)
            for k in range(2):
                n = near[d][k]
                product = dot(tile(d, 1 + k), cols[t, jnp.clip(n, 0, 3)]).astype(bf16)
                out[3 * d + 1 + k] = jnp.where(n >= 2, product, tile(d, 1 + k))
            out[6 + d] = cols[t, d]
            out[8 + d] = block(d)


def interior_kernel(
    rows, total, offs_hbm, aggs_hbm, tiles_hbm, basis_hbm, prol_hbm, early_ref, mid_ref, pc_ref,
    offs, aggs, tiles, basis, prol, cols, acc, tile_sems, basis_sems, out_sems, small_sems,
):
    own = place_of(rows)
    units = rows // GRP
    start, offs_in = offsets_copy(own, total, offs_hbm, offs, small_sems.at[0])
    aggs_in = pltpu.make_async_copy(aggs_hbm, aggs, small_sems.at[1])

    def part_of(u):
        return pl.ds(u * GRP, GRP)

    def tile_copy(u):
        return pltpu.make_async_copy(tiles_hbm.at[part_of(u)], tiles.at[part_of(u)], tile_sems.at[u])

    def basis_copy(u):
        return pltpu.make_async_copy(basis_hbm.at[part_of(u)], basis.at[part_of(u)], basis_sems.at[u])

    def out_copy(u):
        return pltpu.make_async_copy(prol.at[part_of(u)], prol_hbm.at[part_of(u)], out_sems.at[u])

    offs_in.start()
    aggs_in.start()
    basis_copy(0).start()
    for u in range(units):
        tile_copy(u).start()
        if u < units - 1:
            basis_copy(u + 1).start()
    acc[...] = jnp.zeros_like(acc)
    offs_in.wait()
    aggs_in.wait()
    basis_copy(0).wait()
    base = aggs[own]
    count = aggs[own + rows - 1] - base + 1

    def agg_of(m):
        return aggs[own + m]

    def near_of(m):
        return [m] + [jnp.clip(m + offs[k, own - start + m], 0, rows - 1) for k in range(2)]

    def smooth(u):
        mine = agg_of(u * GRP)
        slot = lax.rem(mine, 2)
        for i in range(GRP):
            m = u * GRP + i
            n = near_of(m)
            row = smooth_row([tiles[m, k] for k in range(3)], [basis[x] for x in n])
            for k in range(3):
                prol[m, k] = row[k]
            p0, p1, p2 = [x.astype(f32) for x in row]
            if 2 <= i < GRP - 2:
                cols[m, slot] = (p0 + p1 + p2).astype(bf16)
                cols[m, 1 - slot] = jnp.zeros_like(row[0])
            else:
                w1, w2 = [jnp.where(agg_of(x) == mine, 1.0, 0.0).astype(f32) for x in n[1:]]
                cols[m, slot] = (p0 + w1 * p1 + w2 * p2).astype(bf16)
                cols[m, 1 - slot] = ((1.0 - w1) * p1 + (1.0 - w2) * p2).astype(bf16)

    def window(w, columns_of):
        left, right = [], []
        for i in range(GRP):
            m = w * GRP - HALF + i
            lhs = wide([tiles[m, k] for k in range(3)])
            right.append(dot(lhs, tall([columns_of(x) for x in near_of(m)])).astype(bf16))
            left.append(columns_of(m))
        return dot_t(tall(left), tall(right))

    def step(w, u):
        low, high = agg_of((w - 1) * GRP), agg_of(w * GRP)

        @pl.when(low == high)
        def _():
            slot = lax.rem(low, 2)
            added = window(w, lambda x: cols[x, slot])
            if u is not None:
                smooth(u)
            acc[low - base, 1] += added

        @pl.when(low != high)
        def _():
            size = tiles.shape[-1]
            added = window(w, lambda x: wide([cols[x, 0], cols[x, 1]]))
            if u is not None:
                smooth(u)
            at = [jnp.where(lax.rem(low, 2) == s, low, high) for s in range(2)]
            for r in range(2):
                for s in range(2):
                    acc[at[r] - base, at[s] - at[r] + 1] += added[
                        r * size : (r + 1) * size, s * size : (s + 1) * size
                    ]

    def arrived(u):
        tile_copy(u).wait()

        @pl.when(u < units - 1)
        def _():
            basis_copy(u + 1).wait()

    for u in range(2):
        arrived(u)
        smooth(u)
        out_copy(u).start()

    def unit(u, carry):
        arrived(u)
        step(u - 1, u)
        out_copy(u).start()
        return carry

    lax.fori_loop(2, units, unit, 0)
    step(units - 1, None)
    first_slot, last_slot = lax.rem(base, 2), lax.rem(agg_of(rows - 1), 2)
    for i in range(4):
        pc_ref[i] = cols[2 + i, first_slot]
        pc_ref[4 + i] = cols[rows - 6 + i, last_slot]
    early_ref[0] = acc[0, 2].astype(bf16)
    early_ref[7] = acc[count - 1, 0].astype(bf16)
    for j in (1, 2):
        kept = jnp.where(j < count - 1, 1.0, 0.0).astype(f32)
        for b in range(3):
            early_ref[3 * j - 2 + b] = (kept * acc[j, b]).astype(bf16)
    mid_ref[0] = acc[0, 1]
    mid_ref[1] = acc[count - 1, 1]
    for u in range(units):
        out_copy(u).wait()


def rim_kernel(
    rows, total, offs_hbm, first_got, second_got, tiles, basis, pc_ref, mid_ref, prol_in,
    prol_hbm, late_ref, offs, first_prol, second_prol, first_cols, second_cols, sems,
):
    own = place_of(rows)
    size = tiles.shape[-1]
    start, offs_in = offsets_copy(own, total, offs_hbm, offs, sems.at[2])
    offs_in.start()
    borders = []
    for step, got, prol, cols in ((0, first_got, first_prol, first_cols), (1, second_got, second_prol, second_cols)):
        side, way = side_of(rows, own, step)

        def tile(f, k, step=step, got=got, side=side, way=way):
            return got[3 * (1 - f) + k] if f < 2 else tiles[step, side * 3 + way * (f - 2), k]

        scales = [row_scale(tile(f, 0)) for f in range(4)]
        for f in range(2):
            cols[f, :, :size] = got[7 - f]
        for i in range(4):
            cols[4 + i, :, size:] = pc_ref[side * 7 + way * i]
            cols[4 + i, :, :size] = jnp.zeros((size, size), bf16)
        borders.append((step, got, prol, cols, side, way, tile, scales))
    offs_in.wait()

    near = []
    for step, got, prol, cols, side, way, tile, scales in borders:

        def near_of(f, side=side, way=way):
            m = own + side * (rows - 1) + way * (f - 2)
            inside = (m >= 0) & (m < total)
            at = jnp.clip(m, 0, total - 1) - start
            return [f + way * jnp.where(inside, offs[k, at], 0) for k in range(2)]

        def basis_of(x, step=step, got=got, side=side, way=way):
            mine = basis[step, side * 5 + way * jnp.clip(x - 2, 0, 5)]
            return jnp.where(x < 2, got[9 - jnp.clip(x, 0, 1)], mine)

        near.append([near_of(f) for f in range(6)])
        for f in (2, 3, 0, 1):
            w1, w2 = [weight(x >= 2) for x in near[step][f]]
            p1, p2 = [
                (scales[f] * dot(tile(f, 1 + k), basis_of(near[step][f][k]))).astype(bf16) for k in range(2)
            ]
            q1, q2 = p1.astype(f32), p2.astype(f32)
            if f >= 2:
                here = basis[step, side * 5 + way * (f - 2)]
                p0 = (here.astype(f32) + scales[f] * dot(tile(f, 0), here)).astype(bf16)
                for k, block in enumerate((p0, p1, p2)):
                    prol[side + way * (f - 2), k] = block
                cols[f, :, size:] = (p0.astype(f32) + w1 * q1 + w2 * q2).astype(bf16)
                cols[f, :, :size] = ((1.0 - w1) * q1 + (1.0 - w2) * q2).astype(bf16)
            else:
                cols[f, :, size:] = (w1 * q1 + w2 * q2).astype(bf16)
    outs = []
    for step, got, prol, cols, side, way, tile, scales in borders:
        outs.append(pltpu.make_async_copy(prol, prol_hbm.at[pl.ds(side * (rows - 2), 2)], sems.at[step]))
        outs[step].start()
    products = []
    for step, got, prol, cols, side, way, tile, scales in borders:
        left, right = [], []
        for f in range(6):
            x1, x2 = near[step][f]
            if f < 2:
                zero = jnp.zeros((size, size), bf16)
                lhs = wide([tile(f, 0)] + [jnp.where(x >= 0, tile(f, 1 + k), zero) for k, x in enumerate((x1, x2))])
                more = sum(jnp.where(x >= 0, zero, tile(f, 1 + k)).astype(f32) for k, x in enumerate((x1, x2)))
                x1, x2 = jnp.clip(x1, 0, 3), jnp.clip(x2, 0, 3)
                product = dot(lhs, tall([cols[x] for x in (f, x1, x2)]))
                product = wide([product[:, :size] + more, product[:, size:]])
            else:
                product = dot(wide([tile(f, k) for k in range(3)]), tall([cols[x] for x in (f, x1, x2)]))
            right.append(product.astype(bf16))
            left.append(cols[f, :, size:])
        products.append(dot_t(tall(left), tall(right)))
    for step, got, prol, cols, side, way, tile, scales in borders:
        late_ref[3 * side] = products[step][:, :size].astype(bf16)
        late_ref[side + 1] = (products[step][:, size:] + mid_ref[side]).astype(bf16)
    for out in outs:
        out.wait()


def place_rows(block, early, late, count):
    block[0, 0] = late[0]
    block[0, 1] = late[1]
    block[0, 2] = early[0]
    for b in range(3):
        block[1, b] = early[1 + b]
        block[2, b] = early[4 + b]
        block[3, b] = jnp.zeros_like(early[0])
    block[count - 1, 0] = early[7]
    block[count - 1, 1] = late[2]
    block[count - 1, 2] = late[3]


def near_kernel(rows, aggs_hbm, early_0, early_1, late_0, late_1, out_hbm, counts, aggs, blocks, sem, sems):
    aggs_in = pltpu.make_async_copy(aggs_hbm, aggs, sem)
    aggs_in.start()
    aggs_in.wait()
    region = lax.axis_index("region")
    copies = []
    for j in range(4):
        source = lax.bitwise_xor(region, j)
        own = (source * lax.axis_size("dev") + lax.axis_index("dev")) * rows
        count = aggs[own + rows - 1] - aggs[own] + 1
        counts[j : j + 1, :] = jnp.full((1, counts.shape[1]), count, jnp.int32)
        if j < 2:
            place_rows(blocks.at[j], (early_0, early_1)[j], (late_0, late_1)[j], count)
            copies.append(
                pltpu.make_async_copy(blocks.at[j], out_hbm.at[pl.ds(source * MOSTA, MOSTA)], sems.at[j])
            )
            copies[j].start()
    for c in copies:
        c.wait()


def far_kernel(counts, early_2, early_3, late_2, late_3, coarse_in, out, blocks, sems):
    region = lax.axis_index("region")
    copies = []
    for j, (early, late) in enumerate(((early_2, late_2), (early_3, late_3))):
        place_rows(blocks.at[j], early, late, counts[2 + j, 0])
        at = lax.bitwise_xor(region, 2 + j) * MOSTA
        copies.append(pltpu.make_async_copy(blocks.at[j], out.at[pl.ds(at, MOSTA)], sems.at[j]))
        copies[j].start()
    for c in copies:
        c.wait()


VM = pl.BlockSpec(memory_space=pltpu.VMEM)
ANY = pl.BlockSpec(memory_space=pl.ANY)
DMA = pltpu.SemaphoreType.DMA


def cost(products, bytes_accessed):
    return pl.CostEstimate(flops=2 * 128**3 * products, bytes_accessed=bytes_accessed, transcendentals=0)


def swap(block, by):
    return lax.ppermute(block, "region", [(i, i ^ by) for i in range(lax.axis_size("region"))])


def local(tile_values, basis_tiles, tile_offsets, aggregate_ids):
    rows, _, size, width = tile_values.shape
    total = tile_offsets.shape[0]
    hbm = lambda x: pltpu.with_memory_space_constraint(x, pltpu.HBM)
    tile_values, basis_tiles, aggregate_ids = hbm(tile_values), hbm(basis_tiles), hbm(aggregate_ids)
    offs_all = hbm(tile_offsets.T)
    block = (size, width)
    sds = jax.ShapeDtypeStruct
    window = pltpu.SMEM((2, 256), jnp.int32)
    ids = pltpu.SMEM((total,), jnp.int32)
    first, middle, last = [pltpu.CompilerParams(vmem_limit_bytes=int(x * 2**20)) for x in LIMITS]
    first_out, second_out, edge_tiles, edge_basis = pl.pallas_call(
        functools.partial(edges_kernel, rows, total),
        out_shape=[pltpu.VMEM(x + block, bf16) for x in ((10,), (10,), (2, 4, 3), (2, 6))],
        in_specs=[ANY, ANY, ANY],
        out_specs=[VM] * 4,
        scratch_shapes=[window, pltpu.VMEM((2, 4, *block), bf16), DMA((5,))],
        compiler_params=first,
        cost_estimate=cost(24, 2 * 10**6),
        name="edges",
    )(offs_all, tile_values, basis_tiles)
    devices = lax.axis_size(AXES)
    first_pairs = [(i, i + 1) for i in range(0, devices - 1, 2)]
    second_pairs = [(i, i + 1) for i in range(1, devices - 1, 2)]
    got = [
        lax.ppermute(x, AXES, pairs + [(j, i) for i, j in pairs])
        for x, pairs in ((first_out, first_pairs), (second_out, second_pairs))
    ]
    prol, early, mid, pc = pl.pallas_call(
        functools.partial(interior_kernel, rows, total),
        out_shape=[
            sds((rows, 3, *block), bf16),
            pltpu.VMEM((8, *block), bf16),
            pltpu.VMEM((2, *block), f32),
            pltpu.VMEM((8, *block), bf16),
        ],
        in_specs=[ANY, ANY, ANY, ANY],
        out_specs=[ANY, VM, VM, VM],
        scratch_shapes=[
            window,
            ids,
            pltpu.VMEM((rows, 3, *block), bf16),
            pltpu.VMEM((rows, *block), bf16),
            pltpu.VMEM((rows, 3, *block), bf16),
            pltpu.VMEM((rows, 2, *block), bf16),
            pltpu.VMEM((MOSTA, 3, *block), f32),
            DMA((rows // GRP,)),
            DMA((rows // GRP,)),
            DMA((rows // GRP,)),
            DMA((2,)),
        ],
        compiler_params=middle,
        cost_estimate=cost(64 * 10, 16 * 10**6),
        name="interior",
    )(offs_all, aggregate_ids, tile_values, basis_tiles)
    early_across, early_beside = swap(early, 2), swap(early, 1)
    prol, late = pl.pallas_call(
        functools.partial(rim_kernel, rows, total),
        out_shape=[sds((rows, 3, *block), bf16), pltpu.VMEM((4, *block), bf16)],
        in_specs=[ANY] + [VM] * 6 + [ANY],
        out_specs=[ANY, VM],
        scratch_shapes=[
            window,
            pltpu.VMEM((2, 3, *block), bf16),
            pltpu.VMEM((2, 3, *block), bf16),
            pltpu.VMEM((8, size, 2 * width), bf16),
            pltpu.VMEM((8, size, 2 * width), bf16),
            DMA((3,)),
        ],
        input_output_aliases={7: 0},
        compiler_params=last,
        cost_estimate=cost(140, 2 * 10**6),
        name="rim",
    )(offs_all, *got, edge_tiles, edge_basis, pc, mid, prol)
    late_across, late_beside = swap(late, 2), swap(late, 1)
    coarse, counts = pl.pallas_call(
        functools.partial(near_kernel, rows),
        out_shape=[sds((4 * MOSTA, 3, *block), bf16), pltpu.VMEM((8, 128), jnp.int32)],
        in_specs=[ANY] + [VM] * 4,
        out_specs=[ANY, VM],
        scratch_shapes=[ids, pltpu.VMEM((2, MOSTA, 3, *block), bf16), DMA, DMA((2,))],
        compiler_params=last,
        cost_estimate=cost(0, 2 * 10**6),
        name="near",
    )(aggregate_ids, early, early_beside, late, late_beside)
    early_across, coarse = lax.optimization_barrier((early_across, coarse))
    early_both, late_both = swap(early_across, 1), swap(late_across, 1)
    coarse = pl.pallas_call(
        far_kernel,
        out_shape=sds((4 * MOSTA, 3, *block), bf16),
        in_specs=[VM] * 5 + [ANY],
        out_specs=ANY,
        scratch_shapes=[pltpu.VMEM((2, MOSTA, 3, *block), bf16), DMA((2,))],
        input_output_aliases={5: 0},
        compiler_params=last,
        cost_estimate=cost(0, 2 * 10**6),
        name="far",
    )(counts, early_across, early_both, late_across, late_both, coarse)
    return prol, coarse


def solution(mesh):
    placed = (P(AXES, None, None, None), P(AXES, None, None), P(), P())
    return jax.shard_map(
        local,
        mesh=mesh,
        in_specs=placed,
        out_specs=(P(AXES, None, None, None), P("dev", None, None, None)),
        check_vma=False,
    )
```

```python
import functools

import jax
import jax.numpy as jnp
from jax import lax
from jax.experimental import pallas as pl
from jax.experimental.pallas import tpu as pltpu
from jax.sharding import PartitionSpec as P

MOSTA = 4
GRP = 8
HALF = 4
damping = 0.6
f32, bf16 = jnp.float32, jnp.bfloat16
AXES = ("region", "dev")
LIMITS = (16.0, 40.0, 16.0)


def row_scale(diagonal_tile):
    size = diagonal_tile.shape[0]
    on = lax.broadcasted_iota(jnp.int32, (size, size), 0) == lax.broadcasted_iota(
        jnp.int32, (size, size), 1
    )
    diag = jnp.sum(jnp.where(on, diagonal_tile.astype(f32), 0.0), axis=1, keepdims=True)
    return -damping * (1.0 / jnp.where(diag == 0.0, 1.0, diag))


def dot(a, b):
    return jnp.dot(a, b, preferred_element_type=f32)


def dot_t(a, b):
    return lax.dot_general(a, b, (((0,), (0,)), ((), ())), preferred_element_type=f32)


def tall(blocks):
    return jnp.concatenate(blocks, axis=0)


def wide(blocks):
    return jnp.concatenate(blocks, axis=1)


def smooth_row(tiles, near):
    scale = row_scale(tiles[0])
    head = near[0].astype(f32) + scale * dot(tiles[0], near[0])
    rest = [scale * dot(tiles[k], near[k]) for k in (1, 2)]
    return [x.astype(bf16) for x in (head, *rest)]


def weight(condition):
    return jnp.where(condition, 1.0, 0.0).astype(f32)


def place_of(rows):
    return (lax.axis_index("region") * lax.axis_size("dev") + lax.axis_index("dev")) * rows


def offsets_copy(own, total, offs_hbm, offs, sem):
    start = pl.multiple_of(jnp.clip((own - 2) // 128 * 128, 0, total - 256), 128)
    return start, pltpu.make_async_copy(offs_hbm.at[:, pl.ds(start, 256)], offs, sem)


def side_of(rows, own, step):
    odd = lax.rem(own // rows, 2)
    side = 1 - odd if step == 0 else odd
    return side, 1 - 2 * side


def edges_kernel(
    rows, total, offs_hbm, tiles_hbm, basis_hbm, first_ref, second_ref, tiles, basis, offs, cols, sems
):
    own = place_of(rows)
    start, offs_in = offsets_copy(own, total, offs_hbm, offs, sems.at[4])
    copies = []
    for t in range(2):
        side, way = side_of(rows, own, t)
        copies.append(
            [
                pltpu.make_async_copy(
                    basis_hbm.at[pl.ds(side * (rows - 6), 6)], basis.at[t], sems.at[2 * t]
                ),
                pltpu.make_async_copy(
                    tiles_hbm.at[pl.ds(side * (rows - 4), 4)], tiles.at[t], sems.at[2 * t + 1]
                ),
            ]
        )
    offs_in.start()
    for group in copies:
        for c in group:
            c.start()
    offs_in.wait()
    for group in copies:
        for c in group:
            c.wait()
    for t, out in enumerate((first_ref, second_ref)):
        side, way = side_of(rows, own, t)

        def tile(d, k, t=t, side=side, way=way):
            return tiles[t, side * 3 + way * d, k]

        def block(d, t=t, side=side, way=way):
            return basis[t, side * 5 + way * d]

        near = [
            [d + way * offs[k, own - start + side * (rows - 1) + way * d] for k in range(2)] for d in range(4)
        ]
        for d in range(4):
            blocks = [block(d)] + [block(jnp.clip(n, 0, 5)) for n in near[d]]
            p0, p1, p2 = smooth_row([tile(d, k) for k in range(3)], blocks)
            w1, w2 = [weight(n >= 0) for n in near[d]]
            cols[t, d] = (p0.astype(f32) + w1 * p1.astype(f32) + w2 * p2.astype(f32)).astype(bf16)
        for d in range(2):
            out[3 * d] = tile(d, 0)
            for k in range(2):
                n = near[d][k]
                product = dot(tile(d, 1 + k), cols[t, jnp.clip(n, 0, 3)]).astype(bf16)
                out[3 * d + 1 + k] = jnp.where(n >= 2, product, tile(d, 1 + k))
            out[6 + d] = cols[t, d]
            out[8 + d] = block(d)


def interior_kernel(
    rows, total, offs_hbm, aggs_hbm, tiles, basis, prol_hbm, early_ref, mid_ref, pc_ref,
    offs, aggs, prol, cols, acc, out_sems, small_sems,
):
    own = place_of(rows)
    units = rows // GRP
    start, offs_in = offsets_copy(own, total, offs_hbm, offs, small_sems.at[0])
    aggs_in = pltpu.make_async_copy(aggs_hbm, aggs, small_sems.at[1])

    def part_of(u):
        return pl.ds(u * GRP, GRP)

    def out_copy(u):
        return pltpu.make_async_copy(prol.at[part_of(u)], prol_hbm.at[part_of(u)], out_sems.at[u])

    offs_in.start()
    aggs_in.start()
    acc[...] = jnp.zeros_like(acc)
    offs_in.wait()
    aggs_in.wait()
    base = aggs[own]
    count = aggs[own + rows - 1] - base + 1

    def agg_of(m):
        return aggs[own + m]

    def near_of(m):
        return [m] + [jnp.clip(m + offs[k, own - start + m], 0, rows - 1) for k in range(2)]

    def smooth(u):
        mine = agg_of(u * GRP)
        slot = lax.rem(mine, 2)
        for i in range(GRP):
            m = u * GRP + i
            n = near_of(m)
            row = smooth_row([tiles[m, k] for k in range(3)], [basis[x] for x in n])
            for k in range(3):
                prol[m, k] = row[k]
            p0, p1, p2 = [x.astype(f32) for x in row]
            if 2 <= i < GRP - 2:
                cols[m, slot] = (p0 + p1 + p2).astype(bf16)
                cols[m, 1 - slot] = jnp.zeros_like(row[0])
            else:
                w1, w2 = [jnp.where(agg_of(x) == mine, 1.0, 0.0).astype(f32) for x in n[1:]]
                cols[m, slot] = (p0 + w1 * p1 + w2 * p2).astype(bf16)
                cols[m, 1 - slot] = ((1.0 - w1) * p1 + (1.0 - w2) * p2).astype(bf16)

    def window(w, columns_of):
        left, right = [], []
        for i in range(GRP):
            m = w * GRP - HALF + i
            lhs = wide([tiles[m, k] for k in range(3)])
            right.append(dot(lhs, tall([columns_of(x) for x in near_of(m)])).astype(bf16))
            left.append(columns_of(m))
        return dot_t(tall(left), tall(right))

    def step(w, u):
        low, high = agg_of((w - 1) * GRP), agg_of(w * GRP)

        @pl.when(low == high)
        def _():
            slot = lax.rem(low, 2)
            added = window(w, lambda x: cols[x, slot])
            if u is not None:
                smooth(u)
            acc[low - base, 1] += added

        @pl.when(low != high)
        def _():
            size = tiles.shape[-1]
            added = window(w, lambda x: wide([cols[x, 0], cols[x, 1]]))
            if u is not None:
                smooth(u)
            at = [jnp.where(lax.rem(low, 2) == s, low, high) for s in range(2)]
            for r in range(2):
                for s in range(2):
                    acc[at[r] - base, at[s] - at[r] + 1] += added[
                        r * size : (r + 1) * size, s * size : (s + 1) * size
                    ]

    for u in range(2):
        smooth(u)
        out_copy(u).start()

    def unit(u, carry):
        step(u - 1, u)
        out_copy(u).start()
        return carry

    lax.fori_loop(2, units, unit, 0)
    step(units - 1, None)
    first_slot, last_slot = lax.rem(base, 2), lax.rem(agg_of(rows - 1), 2)
    for i in range(4):
        pc_ref[i] = cols[2 + i, first_slot]
        pc_ref[4 + i] = cols[rows - 6 + i, last_slot]
    early_ref[0] = acc[0, 2].astype(bf16)
    early_ref[7] = acc[count - 1, 0].astype(bf16)
    for j in (1, 2):
        kept = jnp.where(j < count - 1, 1.0, 0.0).astype(f32)
        for b in range(3):
            early_ref[3 * j - 2 + b] = (kept * acc[j, b]).astype(bf16)
    mid_ref[0] = acc[0, 1]
    mid_ref[1] = acc[count - 1, 1]
    for u in range(units):
        out_copy(u).wait()


def rim_kernel(
    rows, total, offs_hbm, first_got, second_got, tiles, basis, pc_ref, mid_ref, prol_in,
    prol_hbm, late_ref, offs, first_prol, second_prol, first_cols, second_cols, sems,
):
    own = place_of(rows)
    size = tiles.shape[-1]
    start, offs_in = offsets_copy(own, total, offs_hbm, offs, sems.at[2])
    offs_in.start()
    borders = []
    for step, got, prol, cols in ((0, first_got, first_prol, first_cols), (1, second_got, second_prol, second_cols)):
        side, way = side_of(rows, own, step)

        def tile(f, k, step=step, got=got, side=side, way=way):
            return got[3 * (1 - f) + k] if f < 2 else tiles[step, side * 3 + way * (f - 2), k]

        scales = [row_scale(tile(f, 0)) for f in range(4)]
        for f in range(2):
            cols[f, :, :size] = got[7 - f]
        for i in range(4):
            cols[4 + i, :, size:] = pc_ref[side * 7 + way * i]
            cols[4 + i, :, :size] = jnp.zeros((size, size), bf16)
        borders.append((step, got, prol, cols, side, way, tile, scales))
    offs_in.wait()

    near = []
    for step, got, prol, cols, side, way, tile, scales in borders:

        def near_of(f, side=side, way=way):
            m = own + side * (rows - 1) + way * (f - 2)
            inside = (m >= 0) & (m < total)
            at = jnp.clip(m, 0, total - 1) - start
            return [f + way * jnp.where(inside, offs[k, at], 0) for k in range(2)]

        def basis_of(x, step=step, got=got, side=side, way=way):
            mine = basis[step, side * 5 + way * jnp.clip(x - 2, 0, 5)]
            return jnp.where(x < 2, got[9 - jnp.clip(x, 0, 1)], mine)

        near.append([near_of(f) for f in range(6)])
        for f in (2, 3, 0, 1):
            w1, w2 = [weight(x >= 2) for x in near[step][f]]
            p1, p2 = [
                (scales[f] * dot(tile(f, 1 + k), basis_of(near[step][f][k]))).astype(bf16) for k in range(2)
            ]
            q1, q2 = p1.astype(f32), p2.astype(f32)
            if f >= 2:
                here = basis[step, side * 5 + way * (f - 2)]
                p0 = (here.astype(f32) + scales[f] * dot(tile(f, 0), here)).astype(bf16)
                for k, block in enumerate((p0, p1, p2)):
                    prol[side + way * (f - 2), k] = block
                cols[f, :, size:] = (p0.astype(f32) + w1 * q1 + w2 * q2).astype(bf16)
                cols[f, :, :size] = ((1.0 - w1) * q1 + (1.0 - w2) * q2).astype(bf16)
            else:
                cols[f, :, size:] = (w1 * q1 + w2 * q2).astype(bf16)
    outs = []
    for step, got, prol, cols, side, way, tile, scales in borders:
        outs.append(pltpu.make_async_copy(prol, prol_hbm.at[pl.ds(side * (rows - 2), 2)], sems.at[step]))
        outs[step].start()
    products = []
    for step, got, prol, cols, side, way, tile, scales in borders:
        left, right = [], []
        for f in range(6):
            x1, x2 = near[step][f]
            if f < 2:
                zero = jnp.zeros((size, size), bf16)
                lhs = wide([tile(f, 0)] + [jnp.where(x >= 0, tile(f, 1 + k), zero) for k, x in enumerate((x1, x2))])
                more = sum(jnp.where(x >= 0, zero, tile(f, 1 + k)).astype(f32) for k, x in enumerate((x1, x2)))
                x1, x2 = jnp.clip(x1, 0, 3), jnp.clip(x2, 0, 3)
                product = dot(lhs, tall([cols[x] for x in (f, x1, x2)]))
                product = wide([product[:, :size] + more, product[:, size:]])
            else:
                product = dot(wide([tile(f, k) for k in range(3)]), tall([cols[x] for x in (f, x1, x2)]))
            right.append(product.astype(bf16))
            left.append(cols[f, :, size:])
        products.append(dot_t(tall(left), tall(right)))
    for step, got, prol, cols, side, way, tile, scales in borders:
        late_ref[3 * side] = products[step][:, :size].astype(bf16)
        late_ref[side + 1] = (products[step][:, size:] + mid_ref[side]).astype(bf16)
    for out in outs:
        out.wait()


def place_rows(block, early, late, count):
    block[0, 0] = late[0]
    block[0, 1] = late[1]
    block[0, 2] = early[0]
    for b in range(3):
        block[1, b] = early[1 + b]
        block[2, b] = early[4 + b]
        block[3, b] = jnp.zeros_like(early[0])
    block[count - 1, 0] = early[7]
    block[count - 1, 1] = late[2]
    block[count - 1, 2] = late[3]


def near_kernel(rows, aggs_hbm, early_0, early_1, late_0, late_1, out_hbm, counts, aggs, blocks, sem, sems):
    aggs_in = pltpu.make_async_copy(aggs_hbm, aggs, sem)
    aggs_in.start()
    aggs_in.wait()
    region = lax.axis_index("region")
    copies = []
    for j in range(4):
        source = lax.bitwise_xor(region, j)
        own = (source * lax.axis_size("dev") + lax.axis_index("dev")) * rows
        count = aggs[own + rows - 1] - aggs[own] + 1
        counts[j : j + 1, :] = jnp.full((1, counts.shape[1]), count, jnp.int32)
        if j < 2:
            place_rows(blocks.at[j], (early_0, early_1)[j], (late_0, late_1)[j], count)
            copies.append(
                pltpu.make_async_copy(blocks.at[j], out_hbm.at[pl.ds(source * MOSTA, MOSTA)], sems.at[j])
            )
            copies[j].start()
    for c in copies:
        c.wait()


def far_kernel(counts, early_2, early_3, late_2, late_3, coarse_in, out, blocks, sems):
    region = lax.axis_index("region")
    copies = []
    for j, (early, late) in enumerate(((early_2, late_2), (early_3, late_3))):
        place_rows(blocks.at[j], early, late, counts[2 + j, 0])
        at = lax.bitwise_xor(region, 2 + j) * MOSTA
        copies.append(pltpu.make_async_copy(blocks.at[j], out.at[pl.ds(at, MOSTA)], sems.at[j]))
        copies[j].start()
    for c in copies:
        c.wait()


VM = pl.BlockSpec(memory_space=pltpu.VMEM)
ANY = pl.BlockSpec(memory_space=pl.ANY)
DMA = pltpu.SemaphoreType.DMA


def cost(products, bytes_accessed):
    return pl.CostEstimate(flops=2 * 128**3 * products, bytes_accessed=bytes_accessed, transcendentals=0)


def swap(block, by):
    return lax.ppermute(block, "region", [(i, i ^ by) for i in range(lax.axis_size("region"))])


def local(tile_values, basis_tiles, tile_offsets, aggregate_ids):
    rows, _, size, width = tile_values.shape
    total = tile_offsets.shape[0]
    hbm = lambda x: pltpu.with_memory_space_constraint(x, pltpu.HBM)
    vmem = lambda x: pltpu.with_memory_space_constraint(x, pltpu.VMEM)
    vmem_tiles, vmem_basis = vmem(tile_values), vmem(basis_tiles)
    tile_values, basis_tiles, aggregate_ids = hbm(tile_values), hbm(basis_tiles), hbm(aggregate_ids)
    offs_all = hbm(tile_offsets.T)
    block = (size, width)
    sds = jax.ShapeDtypeStruct
    window = pltpu.SMEM((2, 256), jnp.int32)
    ids = pltpu.SMEM((total,), jnp.int32)
    first, middle, last = [pltpu.CompilerParams(vmem_limit_bytes=int(x * 2**20)) for x in LIMITS]
    first_out, second_out, edge_tiles, edge_basis = pl.pallas_call(
        functools.partial(edges_kernel, rows, total),
        out_shape=[pltpu.VMEM(x + block, bf16) for x in ((10,), (10,), (2, 4, 3), (2, 6))],
        in_specs=[ANY, ANY, ANY],
        out_specs=[VM] * 4,
        scratch_shapes=[window, pltpu.VMEM((2, 4, *block), bf16), DMA((5,))],
        compiler_params=first,
        cost_estimate=cost(24, 2 * 10**6),
        name="edges",
    )(offs_all, tile_values, basis_tiles)
    devices = lax.axis_size(AXES)
    first_pairs = [(i, i + 1) for i in range(0, devices - 1, 2)]
    second_pairs = [(i, i + 1) for i in range(1, devices - 1, 2)]
    got = [
        lax.ppermute(x, AXES, pairs + [(j, i) for i, j in pairs])
        for x, pairs in ((first_out, first_pairs), (second_out, second_pairs))
    ]
    prol, early, mid, pc = pl.pallas_call(
        functools.partial(interior_kernel, rows, total),
        out_shape=[
            sds((rows, 3, *block), bf16),
            pltpu.VMEM((8, *block), bf16),
            pltpu.VMEM((2, *block), f32),
            pltpu.VMEM((8, *block), bf16),
        ],
        in_specs=[ANY, ANY, VM, VM],
        out_specs=[ANY, VM, VM, VM],
        scratch_shapes=[
            window,
            ids,
            pltpu.VMEM((rows, 3, *block), bf16),
            pltpu.VMEM((rows, 2, *block), bf16),
            pltpu.VMEM((MOSTA, 3, *block), f32),
            DMA((rows // GRP,)),
            DMA((2,)),
        ],
        compiler_params=middle,
        cost_estimate=cost(64 * 10, 16 * 10**6),
        name="interior",
    )(offs_all, aggregate_ids, vmem_tiles, vmem_basis)
    early_across, early_beside = swap(early, 2), swap(early, 1)
    prol, late = pl.pallas_call(
        functools.partial(rim_kernel, rows, total),
        out_shape=[sds((rows, 3, *block), bf16), pltpu.VMEM((4, *block), bf16)],
        in_specs=[ANY] + [VM] * 6 + [ANY],
        out_specs=[ANY, VM],
        scratch_shapes=[
            window,
            pltpu.VMEM((2, 3, *block), bf16),
            pltpu.VMEM((2, 3, *block), bf16),
            pltpu.VMEM((8, size, 2 * width), bf16),
            pltpu.VMEM((8, size, 2 * width), bf16),
            DMA((3,)),
        ],
        input_output_aliases={7: 0},
        compiler_params=last,
        cost_estimate=cost(140, 2 * 10**6),
        name="rim",
    )(offs_all, *got, edge_tiles, edge_basis, pc, mid, prol)
    late_across, late_beside = swap(late, 2), swap(late, 1)
    coarse, counts = pl.pallas_call(
        functools.partial(near_kernel, rows),
        out_shape=[sds((4 * MOSTA, 3, *block), bf16), pltpu.VMEM((8, 128), jnp.int32)],
        in_specs=[ANY] + [VM] * 4,
        out_specs=[ANY, VM],
        scratch_shapes=[ids, pltpu.VMEM((2, MOSTA, 3, *block), bf16), DMA, DMA((2,))],
        compiler_params=last,
        cost_estimate=cost(0, 2 * 10**6),
        name="near",
    )(aggregate_ids, early, early_beside, late, late_beside)
    early_across, coarse = lax.optimization_barrier((early_across, coarse))
    early_both, late_both = swap(early_across, 1), swap(late_across, 1)
    coarse = pl.pallas_call(
        far_kernel,
        out_shape=sds((4 * MOSTA, 3, *block), bf16),
        in_specs=[VM] * 5 + [ANY],
        out_specs=ANY,
        scratch_shapes=[pltpu.VMEM((2, MOSTA, 3, *block), bf16), DMA((2,))],
        input_output_aliases={5: 0},
        compiler_params=last,
        cost_estimate=cost(0, 2 * 10**6),
        name="far",
    )(counts, early_across, early_both, late_across, late_both, coarse)
    return prol, coarse


def solution(mesh):
    placed = (P(AXES, None, None, None), P(AXES, None, None), P(), P())
    return jax.shard_map(
        local,
        mesh=mesh,
        in_specs=placed,
        out_specs=(P(AXES, None, None, None), P("dev", None, None, None)),
        check_vma=False,
    )
```

```python
import functools

import jax
import jax.numpy as jnp
from jax import lax
from jax.experimental import pallas as pl
from jax.experimental.pallas import tpu as pltpu
from jax.sharding import PartitionSpec as P

MOSTA = 4
GRP = 8
HALF = 4
damping = 0.6
f32, bf16 = jnp.float32, jnp.bfloat16
AXES = ("region", "dev")
LIMITS = (16.0, 40.0, 16.0)


def row_scale(diagonal_tile):
    size = diagonal_tile.shape[0]
    on = lax.broadcasted_iota(jnp.int32, (size, size), 0) == lax.broadcasted_iota(
        jnp.int32, (size, size), 1
    )
    diag = jnp.sum(jnp.where(on, diagonal_tile.astype(f32), 0.0), axis=1, keepdims=True)
    return -damping * (1.0 / jnp.where(diag == 0.0, 1.0, diag))


def dot(a, b):
    return jnp.dot(a, b, preferred_element_type=f32)


def dot_t(a, b):
    return lax.dot_general(a, b, (((0,), (0,)), ((), ())), preferred_element_type=f32)


def tall(blocks):
    return jnp.concatenate(blocks, axis=0)


def wide(blocks):
    return jnp.concatenate(blocks, axis=1)


def smooth_row(tiles, near):
    scale = row_scale(tiles[0])
    head = near[0].astype(f32) + scale * dot(tiles[0], near[0])
    rest = [scale * dot(tiles[k], near[k]) for k in (1, 2)]
    return [x.astype(bf16) for x in (head, *rest)]


def weight(condition):
    return jnp.where(condition, 1.0, 0.0).astype(f32)


def place_of(rows):
    return (lax.axis_index("region") * lax.axis_size("dev") + lax.axis_index("dev")) * rows


def offsets_copy(own, total, offs_hbm, offs, sem):
    start = pl.multiple_of(jnp.clip((own - 2) // 128 * 128, 0, total - 256), 128)
    return start, pltpu.make_async_copy(offs_hbm.at[:, pl.ds(start, 256)], offs, sem)


def side_of(rows, own, step):
    odd = lax.rem(own // rows, 2)
    side = 1 - odd if step == 0 else odd
    return side, 1 - 2 * side


def edges_kernel(
    rows, total, offs_hbm, tiles_hbm, basis_hbm, first_ref, second_ref, tiles, basis, offs, cols, sems
):
    own = place_of(rows)
    start, offs_in = offsets_copy(own, total, offs_hbm, offs, sems.at[4])
    copies = []
    for t in range(2):
        side, way = side_of(rows, own, t)
        copies.append(
            [
                pltpu.make_async_copy(
                    basis_hbm.at[pl.ds(side * (rows - 6), 6)], basis.at[t], sems.at[2 * t]
                ),
                pltpu.make_async_copy(
                    tiles_hbm.at[pl.ds(side * (rows - 4), 4)], tiles.at[t], sems.at[2 * t + 1]
                ),
            ]
        )
    offs_in.start()
    for group in copies:
        for c in group:
            c.start()
    offs_in.wait()
    for t, out in enumerate((first_ref, second_ref)):
        side, way = side_of(rows, own, t)
        for c in copies[t]:
            c.wait()

        def tile(d, k, t=t, side=side, way=way):
            return tiles[t, side * 3 + way * d, k]

        def block(d, t=t, side=side, way=way):
            return basis[t, side * 5 + way * d]

        near = [
            [d + way * offs[k, own - start + side * (rows - 1) + way * d] for k in range(2)] for d in range(4)
        ]
        for d in range(4):
            blocks = [block(d)] + [block(jnp.clip(n, 0, 5)) for n in near[d]]
            p0, p1, p2 = smooth_row([tile(d, k) for k in range(3)], blocks)
            w1, w2 = [weight(n >= 0) for n in near[d]]
            cols[t, d] = (p0.astype(f32) + w1 * p1.astype(f32) + w2 * p2.astype(f32)).astype(bf16)
        for d in range(2):
            out[3 * d] = tile(d, 0)
            for k in range(2):
                n = near[d][k]
                product = dot(tile(d, 1 + k), cols[t, jnp.clip(n, 0, 3)]).astype(bf16)
                out[3 * d + 1 + k] = jnp.where(n >= 2, product, tile(d, 1 + k))
            out[6 + d] = cols[t, d]
            out[8 + d] = block(d)


def interior_kernel(
    rows, total, offs_hbm, aggs_hbm, tiles, basis, prol_hbm, early_ref, mid_ref, pc_ref,
    offs, aggs, prol, cols, acc, out_sems, small_sems,
):
    own = place_of(rows)
    units = rows // GRP
    start, offs_in = offsets_copy(own, total, offs_hbm, offs, small_sems.at[0])
    aggs_in = pltpu.make_async_copy(aggs_hbm, aggs, small_sems.at[1])

    def part_of(u):
        return pl.ds(u * GRP, GRP)

    def out_copy(u):
        return pltpu.make_async_copy(prol.at[part_of(u)], prol_hbm.at[part_of(u)], out_sems.at[u])

    offs_in.start()
    aggs_in.start()
    acc[...] = jnp.zeros_like(acc)
    offs_in.wait()
    aggs_in.wait()
    base = aggs[own]
    count = aggs[own + rows - 1] - base + 1

    def agg_of(m):
        return aggs[own + m]

    def near_of(m):
        return [m] + [jnp.clip(m + offs[k, own - start + m], 0, rows - 1) for k in range(2)]

    def smooth(u):
        mine = agg_of(u * GRP)
        slot = lax.rem(mine, 2)
        for i in range(GRP):
            m = u * GRP + i
            n = near_of(m)
            row = smooth_row([tiles[m, k] for k in range(3)], [basis[x] for x in n])
            for k in range(3):
                prol[m, k] = row[k]
            p0, p1, p2 = [x.astype(f32) for x in row]
            if 2 <= i < GRP - 2:
                cols[m, slot] = (p0 + p1 + p2).astype(bf16)
                cols[m, 1 - slot] = jnp.zeros_like(row[0])
            else:
                w1, w2 = [jnp.where(agg_of(x) == mine, 1.0, 0.0).astype(f32) for x in n[1:]]
                cols[m, slot] = (p0 + w1 * p1 + w2 * p2).astype(bf16)
                cols[m, 1 - slot] = ((1.0 - w1) * p1 + (1.0 - w2) * p2).astype(bf16)

    def window(w, columns_of):
        left, right = [], []
        for i in range(GRP):
            m = w * GRP - HALF + i
            lhs = wide([tiles[m, k] for k in range(3)])
            right.append(dot(lhs, tall([columns_of(x) for x in near_of(m)])).astype(bf16))
            left.append(columns_of(m))
        return dot_t(tall(left), tall(right))

    def step(w, u):
        low, high = agg_of((w - 1) * GRP), agg_of(w * GRP)

        @pl.when(low == high)
        def _():
            slot = lax.rem(low, 2)
            added = window(w, lambda x: cols[x, slot])
            if u is not None:
                smooth(u)
            acc[low - base, 1] += added

        @pl.when(low != high)
        def _():
            size = tiles.shape[-1]
            added = window(w, lambda x: wide([cols[x, 0], cols[x, 1]]))
            if u is not None:
                smooth(u)
            at = [jnp.where(lax.rem(low, 2) == s, low, high) for s in range(2)]
            for r in range(2):
                for s in range(2):
                    acc[at[r] - base, at[s] - at[r] + 1] += added[
                        r * size : (r + 1) * size, s * size : (s + 1) * size
                    ]

    for u in range(2):
        smooth(u)
        out_copy(u).start()

    def unit(u, carry):
        step(u - 1, u)
        out_copy(u).start()
        return carry

    lax.fori_loop(2, units, unit, 0)
    step(units - 1, None)
    first_slot, last_slot = lax.rem(base, 2), lax.rem(agg_of(rows - 1), 2)
    for i in range(4):
        pc_ref[i] = cols[2 + i, first_slot]
        pc_ref[4 + i] = cols[rows - 6 + i, last_slot]
    early_ref[0] = acc[0, 2].astype(bf16)
    early_ref[7] = acc[count - 1, 0].astype(bf16)
    for j in (1, 2):
        kept = jnp.where(j < count - 1, 1.0, 0.0).astype(f32)
        for b in range(3):
            early_ref[3 * j - 2 + b] = (kept * acc[j, b]).astype(bf16)
    mid_ref[0] = acc[0, 1]
    mid_ref[1] = acc[count - 1, 1]
    for u in range(units):
        out_copy(u).wait()


def rim_kernel(
    rows, total, offs_hbm, first_got, second_got, tiles, basis, pc_ref, mid_ref, prol_in,
    prol_hbm, late_ref, offs, first_prol, second_prol, first_cols, second_cols, sems,
):
    own = place_of(rows)
    size = tiles.shape[-1]
    start, offs_in = offsets_copy(own, total, offs_hbm, offs, sems.at[2])
    offs_in.start()
    borders = []
    for step, got, prol, cols in ((0, first_got, first_prol, first_cols), (1, second_got, second_prol, second_cols)):
        side, way = side_of(rows, own, step)

        def tile(f, k, step=step, got=got, side=side, way=way):
            return got[3 * (1 - f) + k] if f < 2 else tiles[step, side * 3 + way * (f - 2), k]

        scales = [row_scale(tile(f, 0)) for f in range(4)]
        for f in range(2):
            cols[f, :, :size] = got[7 - f]
        for i in range(4):
            cols[4 + i, :, size:] = pc_ref[side * 7 + way * i]
            cols[4 + i, :, :size] = jnp.zeros((size, size), bf16)
        borders.append((step, got, prol, cols, side, way, tile, scales))
    offs_in.wait()

    near = []
    for step, got, prol, cols, side, way, tile, scales in borders:

        def near_of(f, side=side, way=way):
            m = own + side * (rows - 1) + way * (f - 2)
            inside = (m >= 0) & (m < total)
            at = jnp.clip(m, 0, total - 1) - start
            return [f + way * jnp.where(inside, offs[k, at], 0) for k in range(2)]

        def basis_of(x, step=step, got=got, side=side, way=way):
            mine = basis[step, side * 5 + way * jnp.clip(x - 2, 0, 5)]
            return jnp.where(x < 2, got[9 - jnp.clip(x, 0, 1)], mine)

        near.append([near_of(f) for f in range(6)])
        for f in (2, 3, 0, 1):
            w1, w2 = [weight(x >= 2) for x in near[step][f]]
            p1, p2 = [
                (scales[f] * dot(tile(f, 1 + k), basis_of(near[step][f][k]))).astype(bf16) for k in range(2)
            ]
            q1, q2 = p1.astype(f32), p2.astype(f32)
            if f >= 2:
                here = basis[step, side * 5 + way * (f - 2)]
                p0 = (here.astype(f32) + scales[f] * dot(tile(f, 0), here)).astype(bf16)
                for k, block in enumerate((p0, p1, p2)):
                    prol[side + way * (f - 2), k] = block
                cols[f, :, size:] = (p0.astype(f32) + w1 * q1 + w2 * q2).astype(bf16)
                cols[f, :, :size] = ((1.0 - w1) * q1 + (1.0 - w2) * q2).astype(bf16)
            else:
                cols[f, :, size:] = (w1 * q1 + w2 * q2).astype(bf16)
    outs = []
    for step, got, prol, cols, side, way, tile, scales in borders:
        outs.append(pltpu.make_async_copy(prol, prol_hbm.at[pl.ds(side * (rows - 2), 2)], sems.at[step]))
        outs[step].start()
    products = []
    for step, got, prol, cols, side, way, tile, scales in borders:
        left, right = [], []
        for f in range(6):
            x1, x2 = near[step][f]
            if f < 2:
                zero = jnp.zeros((size, size), bf16)
                lhs = wide([tile(f, 0)] + [jnp.where(x >= 0, tile(f, 1 + k), zero) for k, x in enumerate((x1, x2))])
                more = sum(jnp.where(x >= 0, zero, tile(f, 1 + k)).astype(f32) for k, x in enumerate((x1, x2)))
                x1, x2 = jnp.clip(x1, 0, 3), jnp.clip(x2, 0, 3)
                product = dot(lhs, tall([cols[x] for x in (f, x1, x2)]))
                product = wide([product[:, :size] + more, product[:, size:]])
            else:
                product = dot(wide([tile(f, k) for k in range(3)]), tall([cols[x] for x in (f, x1, x2)]))
            right.append(product.astype(bf16))
            left.append(cols[f, :, size:])
        products.append(dot_t(tall(left), tall(right)))
    for step, got, prol, cols, side, way, tile, scales in borders:
        late_ref[3 * side] = products[step][:, :size].astype(bf16)
        late_ref[side + 1] = (products[step][:, size:] + mid_ref[side]).astype(bf16)
    for out in outs:
        out.wait()


def place_rows(block, early, late, count):
    block[0, 0] = late[0]
    block[0, 1] = late[1]
    block[0, 2] = early[0]
    for b in range(3):
        block[1, b] = early[1 + b]
        block[2, b] = early[4 + b]
        block[3, b] = jnp.zeros_like(early[0])
    block[count - 1, 0] = early[7]
    block[count - 1, 1] = late[2]
    block[count - 1, 2] = late[3]


def near_kernel(rows, aggs_hbm, early_0, early_1, late_0, late_1, out_hbm, counts, aggs, blocks, sem, sems):
    aggs_in = pltpu.make_async_copy(aggs_hbm, aggs, sem)
    aggs_in.start()
    aggs_in.wait()
    region = lax.axis_index("region")
    copies = []
    for j in range(4):
        source = lax.bitwise_xor(region, j)
        own = (source * lax.axis_size("dev") + lax.axis_index("dev")) * rows
        count = aggs[own + rows - 1] - aggs[own] + 1
        counts[j : j + 1, :] = jnp.full((1, counts.shape[1]), count, jnp.int32)
        if j < 2:
            place_rows(blocks.at[j], (early_0, early_1)[j], (late_0, late_1)[j], count)
            copies.append(
                pltpu.make_async_copy(blocks.at[j], out_hbm.at[pl.ds(source * MOSTA, MOSTA)], sems.at[j])
            )
            copies[j].start()
    for c in copies:
        c.wait()


def far_kernel(counts, early_2, early_3, late_2, late_3, coarse_in, out, blocks, sems):
    region = lax.axis_index("region")
    copies = []
    for j, (early, late) in enumerate(((early_2, late_2), (early_3, late_3))):
        place_rows(blocks.at[j], early, late, counts[2 + j, 0])
        at = lax.bitwise_xor(region, 2 + j) * MOSTA
        copies.append(pltpu.make_async_copy(blocks.at[j], out.at[pl.ds(at, MOSTA)], sems.at[j]))
        copies[j].start()
    for c in copies:
        c.wait()


VM = pl.BlockSpec(memory_space=pltpu.VMEM)
ANY = pl.BlockSpec(memory_space=pl.ANY)
DMA = pltpu.SemaphoreType.DMA


def cost(products, bytes_accessed):
    return pl.CostEstimate(flops=2 * 128**3 * products, bytes_accessed=bytes_accessed, transcendentals=0)


def swap(block, by):
    return lax.ppermute(block, "region", [(i, i ^ by) for i in range(lax.axis_size("region"))])


def local(tile_values, basis_tiles, tile_offsets, aggregate_ids):
    rows, _, size, width = tile_values.shape
    total = tile_offsets.shape[0]
    hbm = lambda x: pltpu.with_memory_space_constraint(x, pltpu.HBM)
    vmem = lambda x: pltpu.with_memory_space_constraint(x, pltpu.VMEM)
    vmem_tiles, vmem_basis = vmem(tile_values), vmem(basis_tiles)
    tile_values, basis_tiles, aggregate_ids = hbm(tile_values), hbm(basis_tiles), hbm(aggregate_ids)
    offs_all = hbm(tile_offsets.T)
    block = (size, width)
    sds = jax.ShapeDtypeStruct
    window = pltpu.SMEM((2, 256), jnp.int32)
    ids = pltpu.SMEM((total,), jnp.int32)
    first, middle, last = [pltpu.CompilerParams(vmem_limit_bytes=int(x * 2**20)) for x in LIMITS]
    first_out, second_out, edge_tiles, edge_basis = pl.pallas_call(
        functools.partial(edges_kernel, rows, total),
        out_shape=[pltpu.VMEM(x + block, bf16) for x in ((10,), (10,), (2, 4, 3), (2, 6))],
        in_specs=[ANY, ANY, ANY],
        out_specs=[VM] * 4,
        scratch_shapes=[window, pltpu.VMEM((2, 4, *block), bf16), DMA((5,))],
        compiler_params=first,
        cost_estimate=cost(24, 2 * 10**6),
        name="edges",
    )(offs_all, tile_values, basis_tiles)
    devices = lax.axis_size(AXES)
    first_pairs = [(i, i + 1) for i in range(0, devices - 1, 2)]
    second_pairs = [(i, i + 1) for i in range(1, devices - 1, 2)]
    got = [
        lax.ppermute(x, AXES, pairs + [(j, i) for i, j in pairs])
        for x, pairs in ((first_out, first_pairs), (second_out, second_pairs))
    ]
    prol, early, mid, pc = pl.pallas_call(
        functools.partial(interior_kernel, rows, total),
        out_shape=[
            sds((rows, 3, *block), bf16),
            pltpu.VMEM((8, *block), bf16),
            pltpu.VMEM((2, *block), f32),
            pltpu.VMEM((8, *block), bf16),
        ],
        in_specs=[ANY, ANY, VM, VM],
        out_specs=[ANY, VM, VM, VM],
        scratch_shapes=[
            window,
            ids,
            pltpu.VMEM((rows, 3, *block), bf16),
            pltpu.VMEM((rows, 2, *block), bf16),
            pltpu.VMEM((MOSTA, 3, *block), f32),
            DMA((rows // GRP,)),
            DMA((2,)),
        ],
        compiler_params=middle,
        cost_estimate=cost(64 * 10, 16 * 10**6),
        name="interior",
    )(offs_all, aggregate_ids, vmem_tiles, vmem_basis)
    early_across, early_beside = swap(early, 2), swap(early, 1)
    prol, late = pl.pallas_call(
        functools.partial(rim_kernel, rows, total),
        out_shape=[sds((rows, 3, *block), bf16), pltpu.VMEM((4, *block), bf16)],
        in_specs=[ANY] + [VM] * 6 + [ANY],
        out_specs=[ANY, VM],
        scratch_shapes=[
            window,
            pltpu.VMEM((2, 3, *block), bf16),
            pltpu.VMEM((2, 3, *block), bf16),
            pltpu.VMEM((8, size, 2 * width), bf16),
            pltpu.VMEM((8, size, 2 * width), bf16),
            DMA((3,)),
        ],
        input_output_aliases={7: 0},
        compiler_params=last,
        cost_estimate=cost(140, 2 * 10**6),
        name="rim",
    )(offs_all, *got, edge_tiles, edge_basis, pc, mid, prol)
    late_across, late_beside = swap(late, 2), swap(late, 1)
    coarse, counts = pl.pallas_call(
        functools.partial(near_kernel, rows),
        out_shape=[sds((4 * MOSTA, 3, *block), bf16), pltpu.VMEM((8, 128), jnp.int32)],
        in_specs=[ANY] + [VM] * 4,
        out_specs=[ANY, VM],
        scratch_shapes=[ids, pltpu.VMEM((2, MOSTA, 3, *block), bf16), DMA, DMA((2,))],
        compiler_params=last,
        cost_estimate=cost(0, 2 * 10**6),
        name="near",
    )(aggregate_ids, early, early_beside, late, late_beside)
    early_across, ignored = lax.optimization_barrier((early_across, late_beside))
    early_both, late_both = swap(early_across, 1), swap(late_across, 1)
    coarse = pl.pallas_call(
        far_kernel,
        out_shape=sds((4 * MOSTA, 3, *block), bf16),
        in_specs=[VM] * 5 + [ANY],
        out_specs=ANY,
        scratch_shapes=[pltpu.VMEM((2, MOSTA, 3, *block), bf16), DMA((2,))],
        input_output_aliases={5: 0},
        compiler_params=last,
        cost_estimate=cost(0, 2 * 10**6),
        name="far",
    )(counts, early_across, early_both, late_across, late_both, coarse)
    return prol, coarse


def solution(mesh):
    placed = (P(AXES, None, None, None), P(AXES, None, None), P(), P())
    return jax.shard_map(
        local,
        mesh=mesh,
        in_specs=placed,
        out_specs=(P(AXES, None, None, None), P("dev", None, None, None)),
        check_vma=False,
    )
```
